32 devices in a mesh: layer: 4 (over y, core), row: 2 (over x), col: 4 (over z).
Axes of the slice: x: 2, y: 2, z: 4, core: 2. Of those that a mesh axis runs over, the one named last changes fastest.
Arguments:
- ancestor: float32 [6144, 6144], P('row', 'col'), may hold values from -6 to 6
- leaf_lower: bfloat16 [4, 8, 6144, 512], P('layer', 'col', 'row'), may hold values from -6 to 6
- leaf_upper: bfloat16 [4, 8, 512, 6144], P('layer', None, 'row', 'col'), may hold values from -6 to 6
- leaf_upper_inv: bfloat16 [4, 8, 512, 512], P('layer', 'col'), may hold values from -1 to 1, as said below
- leaf_lower_inv: bfloat16 [4, 8, 512, 512], P('layer'), may hold values from -1 to 2, as said below
- leaf_pivots: int32 [4, 8, 512], P('layer'), may hold values from 0 to 511, each once within a row
- leaf_tiles: int32 [4, 8, 24, 24], P('layer'), may hold values 0 or 1
- anc_upper_inv: bfloat16 [512, 512], replicated, may hold values from -1 to 1, as said below
- anc_lower_inv: bfloat16 [512, 512], replicated, may hold values from -1 to 2, as said below
- anc_pivots: int32 [512], replicated, may hold values from 0 to 511, each once
- anc_tiles: int32 [24, 24], replicated, may hold values 0 or 1
Outputs:
- anc_lower: bfloat16 [6144, 512], P('row')
- anc_upper: bfloat16 [512, 6144], P(None, 'col')
- schur: float32 [6144, 6144], P('row', 'col')
The draws below stay inside these ranges and needn't reach their ends.
Inputs may be any that keep to these rules, and one draw needn't show every extreme that they name: leaf_upper_inv[l,k] is upper triangular with positive diagonal. leaf_lower_inv[l,k] is lower triangular with positive diagonal. `anc_upper_inv`: upper triangular with positive diagonal. `anc_lower_inv`: lower triangular with positive diagonal.
All inputs are finite; a program needn't handle non-finite values. No bound on the sum of `leaf_tiles` on one device may be relied on, other than what follows from the above.
Results may differ from the reference program's by a relative error of at most 0.0085.
Values may be sent and summed in bfloat16 or wider, within the bound.
No kernel may reach another device: no remote copies, remote signals or barrier semaphores. Data moves between devices by JAX's collectives and lax.ppermute only.
A program may use at most 320 MiB of HBM per device.

```python
import jax
import jax.numpy as jnp

NA = 6144
W = 512
TB = 256
LAYERS = 4
LEAVES = 8
RB = 3072
PB = 256
NT = 24


def triangle(key, lead, lower_side):
    first, second = jax.random.split(key)
    shape = lead + (W, W)
    offdiag = jnp.clip(jax.random.normal(first, shape, jnp.float32), -6.0, 6.0)
    diagonal = jnp.exp(jax.random.uniform(second, lead + (W,), jnp.float32, jnp.log(0.5), jnp.log(2.0)))
    identity = jnp.eye(W, dtype=jnp.float32)
    if lower_side:
        matrix = jnp.tril(offdiag, -1) / jnp.sqrt(W * 1.0) + diagonal[..., None] * identity
    else:
        matrix = jnp.triu(offdiag, 1) / (W * 1.0) + diagonal[..., None] * identity / jnp.sqrt(W * 1.0)
    return matrix.astype(jnp.bfloat16)


def draw_leaf_upper_inv(key, part):
    return triangle(jax.random.fold_in(key, 11), (LAYERS, LEAVES), False)


def draw_leaf_lower_inv(key, part):
    return triangle(jax.random.fold_in(key, 12), (LAYERS, LEAVES), True)


def draw_anc_upper_inv(key, part):
    return triangle(jax.random.fold_in(key, 13), (), False)


def draw_anc_lower_inv(key, part):
    return triangle(jax.random.fold_in(key, 14), (), True)


def set_ends(values, own_key, least, largest):
    spot = [jax.random.randint(jax.random.fold_in(own_key, axis), (), 0, length) for axis, length in enumerate(values.shape)]
    main_axis = values.shape.index(max(values.shape))
    next_to = spot[:main_axis] + [(spot[main_axis] + 1) % values.shape[main_axis]] + spot[main_axis + 1:]
    return values.at[tuple(spot)].set(least).at[tuple(next_to)].set(largest)


def levels(rng, shape, pieces, smallest, top_value):
    def one(axis_at, shards_of):
        heights = jax.random.uniform(jax.random.fold_in(jax.random.fold_in(rng, 6), axis_at), (shards_of,), jnp.float32, smallest / len(pieces), top_value / len(pieces))
        return jnp.repeat(jnp.exp(heights), shape[axis_at] // shards_of).reshape((-1,) + (1,) * (len(shape) - axis_at - 1))

    factor_of = one(*pieces[0])
    for cut in pieces[1:]:
        factor_of = factor_of * one(*cut)
    return factor_of


def normal_values(stream_key, extent, scale, limit, pieces=(), kind=jnp.bfloat16):
    entries = scale * jax.random.normal(stream_key, extent, jnp.float32)
    if pieces:
        entries = entries * levels(stream_key, extent, pieces, -0.22, 0.18)
    return jnp.clip(entries, -limit, limit).astype(kind)


def setup_inputs(seed: int = 0) -> dict:
    arg_keys = jax.random.split(jax.random.key(seed), 12)
    ancestor = normal_values(arg_keys[0], (NA, NA), 1.0, 6.0, ((0, 2), (1, 4)), jnp.float32)
    leaf_lower = normal_values(arg_keys[1], (LAYERS, LEAVES, NA, W), 1.0, 6.0, ((0, 4), (1, 4), (2, 2)))
    leaf_upper = normal_values(arg_keys[2], (LAYERS, LEAVES, W, NA), 1.0, 6.0, ((0, 4), (2, 2), (3, 4)))
    leaf_upper_inv = draw_leaf_upper_inv(jax.random.fold_in(arg_keys[11], 71), 0)
    leaf_lower_inv = draw_leaf_lower_inv(jax.random.fold_in(arg_keys[11], 71), 0)
    leaf_pivots = jax.vmap(lambda own: jax.random.permutation(own, W))(jax.random.split(arg_keys[5], LAYERS * LEAVES)).reshape((LAYERS, LEAVES, W)).astype(jnp.int32)
    leaf_tiles = set_ends((jax.random.randint(arg_keys[6], (LAYERS, LEAVES, NT, NT), 0, 2) < 1).astype(jnp.int32), jax.random.fold_in(arg_keys[6], 1), 0, 1)
    anc_upper_inv = draw_anc_upper_inv(jax.random.fold_in(arg_keys[11], 71), 0)
    anc_lower_inv = draw_anc_lower_inv(jax.random.fold_in(arg_keys[11], 71), 0)
    anc_pivots = jax.random.permutation(arg_keys[9], W).astype(jnp.int32)
    anc_tiles = set_ends((jax.random.randint(arg_keys[10], (NT, NT), 0, 2) < 1).astype(jnp.int32), jax.random.fold_in(arg_keys[10], 1), 0, 1)
    return {"ancestor": ancestor, "leaf_lower": leaf_lower, "leaf_upper": leaf_upper, "leaf_upper_inv": leaf_upper_inv, "leaf_lower_inv": leaf_lower_inv, "leaf_pivots": leaf_pivots, "leaf_tiles": leaf_tiles, "anc_upper_inv": anc_upper_inv, "anc_lower_inv": anc_lower_inv, "anc_pivots": anc_pivots, "anc_tiles": anc_tiles}


def tile_mask(tiles):
    expanded = jnp.repeat(jnp.repeat(tiles, TB, axis=0), TB, axis=1)
    return expanded.astype(jnp.float32)


def reference(ancestor, leaf_lower, leaf_upper, leaf_upper_inv, leaf_lower_inv, leaf_pivots, leaf_tiles, anc_upper_inv, anc_lower_inv, anc_pivots, anc_tiles):
    total = jnp.zeros((NA, NA), jnp.float32)
    for layer_index in range(LAYERS):
        for leaf_index in range(LEAVES):
            lower = jnp.dot(leaf_lower[layer_index, leaf_index], leaf_upper_inv[layer_index, leaf_index], preferred_element_type=jnp.float32).astype(jnp.bfloat16)
            permuted = jnp.take(leaf_upper[layer_index, leaf_index], leaf_pivots[layer_index, leaf_index], axis=0)
            upper = jnp.dot(leaf_lower_inv[layer_index, leaf_index], permuted, preferred_element_type=jnp.float32).astype(jnp.bfloat16)
            update = jnp.dot(lower, upper, preferred_element_type=jnp.float32)
            total = total + tile_mask(leaf_tiles[layer_index, leaf_index]) * update
    a_sum = ancestor + total
    blocks = NA // RB
    row_index = (jnp.arange(blocks, dtype=jnp.int32)[:, None] * RB + jnp.arange(PB, dtype=jnp.int32)[None, :]).reshape(-1)
    pivot_rows = jnp.take(a_sum, row_index, axis=0).astype(jnp.bfloat16)
    permuted = jnp.take(pivot_rows, anc_pivots, axis=0)
    anc_upper = jnp.dot(anc_lower_inv, permuted, preferred_element_type=jnp.float32).astype(jnp.bfloat16)
    columns = a_sum[:, :W].astype(jnp.bfloat16)
    anc_lower = jnp.dot(columns, anc_upper_inv, preferred_element_type=jnp.float32).astype(jnp.bfloat16)
    schur = a_sum - tile_mask(anc_tiles) * jnp.dot(anc_lower, anc_upper, preferred_element_type=jnp.float32)
    return anc_lower, anc_upper, schur
```

```python
import functools

import jax
import jax.numpy as jnp
from jax import lax
from jax.experimental import pallas as pl
from jax.experimental.pallas import tpu as pltpu
from jax.sharding import PartitionSpec as P

BF = jnp.bfloat16
F32 = jnp.float32
MIB = 1024 * 1024
SWAP = [(0, 1), (1, 0)]
CORE = [(0, 1), (1, 0), (2, 3), (3, 2)]
YPAIR = [(0, 2), (2, 0), (1, 3), (3, 1)]
BUDDY = [(0, 1), (1, 0), (2, 3), (3, 2)]
PIECE = (0, 2, 1, 3)


def dot(a, b):
    return jnp.dot(a, b, preferred_element_type=F32)


def plain(
    ancestor, leaf_lower, leaf_upper, leaf_upper_inv, leaf_lower_inv, leaf_pivots, leaf_tiles,
    anc_upper_inv, anc_lower_inv, anc_pivots, anc_tiles, *, order,
):
    row_count, col_count = ancestor.shape
    panel_rows = leaf_upper.shape[2]
    width = leaf_lower.shape[-1]
    nt = leaf_tiles.shape[-1]
    tb = order // nt

    def onehot_tiles(first, count):
        tile = (first + jnp.arange(count, dtype=jnp.int32)) // tb
        return (tile[:, None] == jnp.arange(nt, dtype=jnp.int32)[None, :]).astype(F32)

    row_onehot = onehot_tiles(lax.axis_index("row") * row_count, row_count)
    col_onehot = onehot_tiles(lax.axis_index("col") * col_count, col_count)
    rows_all = lax.all_gather(leaf_upper[0], "row", axis=1, tiled=True)
    permuted = jnp.take_along_axis(rows_all, leaf_pivots[0][:, :, None], axis=1)
    upper_all = jnp.einsum("kij,kjc->kic", leaf_lower_inv[0], permuted, preferred_element_type=F32).astype(BF)
    own_lower = jnp.einsum("jrw,jwv->jrv", leaf_lower[0], leaf_upper_inv[0], preferred_element_type=F32).astype(BF)
    masks = jnp.einsum("rt,mts,cs->mrc", row_onehot, leaf_tiles[0].astype(F32), col_onehot)
    products = jnp.einsum(
        "mrw,mwc->mrc", lax.all_gather(own_lower, "col", axis=0, tiled=True), upper_all, preferred_element_type=F32
    )
    a_sum = ancestor + lax.psum(jnp.sum(masks * products, axis=0), "layer")
    gathered = lax.all_gather(a_sum[:panel_rows].astype(BF), "row", axis=0, tiled=True)
    anc_upper = dot(anc_lower_inv, jnp.take(gathered, anc_pivots, axis=0)).astype(BF)
    panel = dot(a_sum[:, :width].astype(BF), anc_upper_inv).astype(BF)
    kept = jnp.where(lax.axis_index("col") == 0, panel, 0).astype(BF)
    anc_lower = lax.psum(kept, "col")
    anc_mask = jnp.einsum("rt,ts,cs->rc", row_onehot, anc_tiles.astype(F32), col_onehot)
    return anc_lower, anc_upper, a_sum - anc_mask * dot(anc_lower, anc_upper)


def upper_kernel(mo_ref, mt_ref, so_ref, st_ref, out_ref):
    total = dot(mo_ref[0], so_ref[0, 0]) + dot(mt_ref[0], st_ref[0, 0])
    out_ref[0, 0] = total.astype(BF)


def make_upper(m_own, m_other, s_own, s_other):
    blocks, pair, half, cw = s_own.shape
    w = m_own.shape[1]
    m_spec = pl.BlockSpec((1, w, half), lambda k, b: (k, 0, 0))
    s_spec = pl.BlockSpec((1, 1, half, cw), lambda k, b: (b, k, 0, 0))
    return pl.pallas_call(
        upper_kernel,
        grid=(pair, blocks),
        in_specs=[m_spec, m_spec, s_spec, s_spec],
        out_specs=pl.BlockSpec((1, 1, w, cw), lambda k, b: (b, k, 0, 0)),
        out_shape=jax.ShapeDtypeStruct((blocks, pair, w, cw), BF),
        cost_estimate=pl.CostEstimate(
            flops=4 * blocks * pair * w * half * cw, transcendentals=0,
            bytes_accessed=2 * (2 * s_own.size + blocks * pair * w * cw),
        ),
        compiler_params=pltpu.CompilerParams(vmem_limit_bytes=16 * MIB),
        name="upper",
    )(m_own, m_other, s_own, s_other)


def product_kernel(place, tiles, low0, low1, up0, up1, keep, send, acc, *, g, c, nt, rt, ct, tb, pair, tj):
    b, j = pl.program_id(0), pl.program_id(1)
    x, z, l = place[0], place[1], place[2]
    odd = lax.rem(z, 2)
    column = jnp.where(b == 0, 3 * odd, 1 + odd) * ct + c * tj + j
    for p, flip in enumerate(PIECE):
        i = jnp.bitwise_xor(l, flip)
        rows = pl.ds(pl.multiple_of(i * tb, tb), tb)
        acc[...] = jnp.zeros_like(acc)
        for low, up, owner in ((low0, up0, z), (low1, up1, jnp.bitwise_xor(z, 1))):
            for k in range(pair):
                leaf = owner * pair + k
                flag = tiles[(leaf * nt + x * rt + g * 4 + i) * nt + column]

                @pl.when(flag != 0)
                def _():
                    acc[...] += dot(low[k, rows, :], up[0, k])

        if p < 2:
            keep[p, 0] = acc[...]
        else:
            send[p - 2, 0] = acc[...].astype(BF)


def products(place, tiles, low0, low1, up0, up1, *, g, c, nt, rt, ct, tb):
    blocks, pair, w, cw = up0.shape
    tj = cw // tb
    rows = 4 * tb
    up_spec = pl.BlockSpec((1, pair, w, tb), lambda b, j, *_: (b, 0, 0, j))
    out_spec = pl.BlockSpec((2, 1, tb, tb), lambda b, j, *_: (0, b, 0, j))
    return pl.pallas_call(
        functools.partial(product_kernel, g=g, c=c, nt=nt, rt=rt, ct=ct, tb=tb, pair=pair, tj=tj),
        grid_spec=pltpu.PrefetchScalarGridSpec(
            num_scalar_prefetch=2,
            grid=(blocks, tj),
            in_specs=[
                pl.BlockSpec((pair, rows, w), lambda b, j, *_: (0, g, 0)),
                pl.BlockSpec((pair, rows, w), lambda b, j, *_: (0, 0, 0)),
                up_spec,
                up_spec,
            ],
            out_specs=[out_spec, out_spec],
            scratch_shapes=[pltpu.VMEM((tb, tb), F32)],
        ),
        out_shape=[
            jax.ShapeDtypeStruct((2, blocks, tb, cw), F32),
            jax.ShapeDtypeStruct((2, blocks, tb, cw), BF),
        ],
        cost_estimate=pl.CostEstimate(
            flops=4 * blocks * pair * rows * w * cw, transcendentals=0, bytes_accessed=24 * MIB,
        ),
        compiler_params=pltpu.CompilerParams(vmem_limit_bytes=24 * MIB),
        name="products",
    )(place, tiles, low0, low1, up0, up1)


def final_kernel(place, tiles, *refs, g, c, nt, rt, ct, tb, tj, first, with_lower):
    anc, tq, ty, tc, au, pq, py, pc = refs[:8]
    outs = refs[8:] if first else refs[8 + (2 if with_lower else 1):]
    p = pl.program_id(0)
    x, z, l = place[0], place[1], place[2]
    flip = jnp.where(p == 0, 0, jnp.where(p == 1, 2, jnp.where(p == 2, 1, 3)))
    i = x * rt + g * 4 + jnp.bitwise_xor(l, flip)

    def work(total, panel):
        if with_lower:
            outs[1][...] = panel
        for j in range(tj):
            cols = slice(j * tb, (j + 1) * tb)
            base = anc[:, cols] + total[:, cols].astype(F32)
            flag = tiles[i * nt + z * ct + c * tj + j] != 0

            @pl.when(flag)
            def _():
                outs[0][:, cols] = base - dot(panel, au[:, cols])

            @pl.when(jnp.logical_not(flag))
            def _():
                outs[0][:, cols] = base

    for q, (t, v) in enumerate(((tq, pq), (ty, py), (tc.at[0], pc.at[0]), (tc.at[1], pc.at[1]))):

        @pl.when(p == q)
        def _():
            work(t[...], v[...])


def final(place, tiles, ancestor, total, au, panel, kept, *, g, c, nt, rt, ct, tb, with_lower):
    rows, cols = ancestor.shape
    tq, ty, tc = total
    pq, py, pc = panel
    cw, w = tq.shape[1], pq.shape[1]
    tj = cw // tb
    first = kept is None

    def whole(shape):
        return pl.BlockSpec(shape, lambda p, *_: (0,) * len(shape))

    def tile_row(p, place):
        flip = jnp.where(p == 0, 0, jnp.where(p == 1, 2, jnp.where(p == 2, 1, 3)))
        return g * 4 + jnp.bitwise_xor(place[2], flip)

    out_specs = [pl.BlockSpec((tb, cw), lambda p, place, *_: (tile_row(p, place), c))]
    out_shape = [jax.ShapeDtypeStruct((rows, cols), F32)]
    if with_lower:
        out_specs.append(pl.BlockSpec((tb, w), lambda p, place, *_: (tile_row(p, place), 0)))
        out_shape.append(jax.ShapeDtypeStruct((rows, w), BF))
    in_specs = [
        pl.BlockSpec((tb, cw), lambda p, place, *_: (tile_row(p, place), c)),
        whole(tq.shape), whole(ty.shape), whole(tc.shape), whole(au.shape),
        whole(pq.shape), whole(py.shape), whole(pc.shape),
    ]
    operands = [ancestor, tq, ty, tc, au, pq, py, pc]
    aliases = {}
    if not first:
        for n in range(len(out_shape)):
            aliases[2 + len(operands)] = n
            operands.append(kept[n])
            in_specs.append(pl.BlockSpec(memory_space=pl.ANY))
    return pl.pallas_call(
        functools.partial(
            final_kernel, g=g, c=c, nt=nt, rt=rt, ct=ct, tb=tb, tj=tj, first=first, with_lower=with_lower
        ),
        grid_spec=pltpu.PrefetchScalarGridSpec(
            num_scalar_prefetch=2, grid=(4,), in_specs=in_specs, out_specs=out_specs
        ),
        out_shape=out_shape,
        input_output_aliases=aliases,
        cost_estimate=pl.CostEstimate(flops=8 * tb * w * cw, transcendentals=0, bytes_accessed=40 * tb * cw),
        compiler_params=pltpu.CompilerParams(vmem_limit_bytes=24 * MIB),
        name="final",
    )(place, tiles, *operands)


def onehot_cols(inverse, pivots, first, count):
    wanted = (first + jnp.arange(count, dtype=jnp.int32))
    picks = (pivots[..., :, None] == wanted).astype(BF)
    return jnp.einsum("...it,...tj->...ij", inverse, picks, preferred_element_type=F32).astype(BF)


def paired(
    ancestor, leaf_lower, leaf_upper, leaf_upper_inv, leaf_lower_inv, leaf_pivots, leaf_tiles,
    anc_upper_inv, anc_lower_inv, anc_pivots, anc_tiles, *, order, split,
):
    rows, cols = ancestor.shape
    pair, w = leaf_lower.shape[1], leaf_lower.shape[-1]
    half = leaf_upper.shape[2]
    nt = leaf_tiles.shape[-1]
    tb = order // nt
    rt, ct = rows // tb, cols // tb
    groups, cw = rows // (4 * tb), cols // split
    x, z, l = lax.axis_index("row"), lax.axis_index("col"), lax.axis_index("layer")
    odd = lax.rem(z, 2)
    is_end = (z == 0) | (z == 3)
    near, far = (z // 2) * 2 * pair, (1 - z // 2) * 2 * pair
    place = jnp.stack([x, z, l]).astype(jnp.int32)
    tiles = leaf_tiles.reshape(-1)
    top_tiles = anc_tiles.reshape(-1)
    shape = dict(nt=nt, rt=rt, ct=ct, tb=tb)

    u = leaf_upper[0]
    ups = {}
    for c in range(split):
        for t in range(2):
            same, other = (odd ^ t) * pair, ((1 - odd) ^ t) * pair

            def part(first):
                return lax.dynamic_slice(u, (first, 0, c * cw), (pair, half, cw))

            p1 = lax.ppermute(part(near + other), "col", [(1, 0), (2, 3)])
            p2 = lax.ppermute(part(far + same), "col", [(0, 2), (3, 1)])
            p3 = lax.ppermute(part(far + other), "col", [(1, 2), (2, 1)])
            own = jnp.stack([jnp.where(is_end, part(near + same), p2), jnp.where(is_end, p1, p3)])
            ups[c, t] = (own, lax.ppermute(own, "row", SWAP))

    lower = jnp.einsum("krw,kwv->krv", leaf_lower[0], leaf_upper_inv[0], preferred_element_type=F32).astype(BF)
    buddy = [lax.ppermute(lower[:, g * 4 * tb:(g + 1) * 4 * tb], "col", BUDDY) for g in range(groups)]

    uppers = {}
    mats = []
    for t in range(2):
        first = near + (odd ^ t) * pair
        inverse = lax.dynamic_slice_in_dim(leaf_lower_inv[0], first, pair, 0)
        pivots = lax.dynamic_slice_in_dim(leaf_pivots[0], first, pair, 0)
        mats.append((onehot_cols(inverse, pivots, x * half, half), onehot_cols(inverse, pivots, (1 - x) * half, half)))
    a_own = onehot_cols(anc_lower_inv, anc_pivots, x * half, half)
    a_other = onehot_cols(anc_lower_inv, anc_pivots, (1 - x) * half, half)
    for (c, t), (own, other) in ups.items():
        uppers[c, t] = make_upper(*mats[t], own, other)

    panels, anc_uppers = {}, {}
    schur, anc_lower = None, None
    for c in range(split):
        for g in range(groups):
            keep, send = products(place, tiles, lower, buddy[g], uppers[c, 0], uppers[c, 1], g=g, c=c, **shape)
            recv = lax.ppermute(send, "layer", CORE)
            crossing = (keep[1] + recv[1].astype(F32)).astype(BF)
            arrived = lax.ppermute(crossing, "layer", YPAIR)
            mine = (keep[0] + recv[0].astype(F32) + arrived.astype(F32)).astype(BF)
            outer, inner = mine[0], mine[1]
            q1 = lax.ppermute(inner, "col", [(0, 1), (3, 2)])
            q2 = lax.ppermute(outer, "col", [(1, 3), (2, 0)])
            q3 = lax.ppermute(inner, "col", [(1, 2), (2, 1)])
            stay = jnp.where(is_end, outer.astype(F32) + q2.astype(F32), q1.astype(F32) + q3.astype(F32))
            tq = stay.astype(BF)
            ty = lax.ppermute(tq, "layer", YPAIR)
            tc = lax.ppermute(jnp.stack([tq, ty]), "layer", CORE)
            if c == 0:
                base = lax.dynamic_slice(ancestor, ((g * 4 + l) * tb, 0), (tb, w))
                pq = dot((base + tq[:, :w].astype(F32)).astype(BF), anc_upper_inv).astype(BF)
                sent = [lax.ppermute(pq, "col", [(0, n)]) for n in (1, 2, 3)]
                pq = jnp.where(z == 0, pq, sent[0] + sent[1] + sent[2])
                py = lax.ppermute(pq, "layer", YPAIR)
                panels[g] = (pq, py, lax.ppermute(jnp.stack([pq, py]), "layer", CORE))
            if g == 0:
                top = jnp.where(l == 0, tq, jnp.where(l == 2, ty, jnp.where(l == 1, tc[0], tc[1])))
                pivot = (ancestor[:tb, c * cw:(c + 1) * cw] + top.astype(F32)).astype(BF)
                swapped = lax.ppermute(pivot, "row", SWAP)
                anc_uppers[c] = (dot(a_own, pivot) + dot(a_other, swapped)).astype(BF)
            kept = None if schur is None else ((schur, anc_lower) if c == 0 else (schur,))
            out = final(
                place, top_tiles, ancestor, (tq, ty, tc), anc_uppers[c], panels[g], kept,
                g=g, c=c, with_lower=c == 0, **shape,
            )
            schur = out[0]
            if c == 0:
                anc_lower = out[1]
    anc_upper = jnp.concatenate([anc_uppers[c] for c in range(split)], axis=1)
    return anc_lower, anc_upper, schur


def solution(mesh):
    sizes = mesh.shape

    def shards(*args):
        ancestor, leaf_lower, leaf_upper, leaf_tiles = args[0], args[1], args[2], args[6]
        rows, cols = ancestor.shape
        order = rows * sizes["row"]
        nt = leaf_tiles.shape[-1]
        tb = order // nt
        w, half = leaf_lower.shape[-1], leaf_upper.shape[2]
        fits = (
            (sizes["layer"], sizes["row"], sizes["col"]) == (4, 2, 4)
            and leaf_lower.shape[0] == 1 and leaf_upper.shape[1] == 4 * leaf_lower.shape[1]
            and order % nt == 0 and rows % (4 * tb) == 0 and cols % (2 * tb) == 0
            and half == tb and tb % 128 == 0 and w <= cols // 2
        )
        if fits:
            return paired(*args, order=order, split=2)
        return plain(*args, order=order)

    return jax.shard_map(
        shards,
        mesh=mesh,
        in_specs=(
            P("row", "col"), P("layer", "col", "row", None), P("layer", None, "row", "col"),
            P("layer", "col", None, None), P("layer", None, None, None), P("layer", None, None),
            P("layer", None, None, None), P(), P(), P(), P(),
        ),
        out_specs=(P("row", None), P(None, "col"), P("row", "col")),
        check_vma=False,
    )
```

```python
import functools

import jax
import jax.numpy as jnp
from jax import lax
from jax.experimental import pallas as pl
from jax.experimental.pallas import tpu as pltpu
from jax.sharding import PartitionSpec as P

BF = jnp.bfloat16
F32 = jnp.float32
MIB = 1024 * 1024
GAP = 2
COST = pl.CostEstimate(flops=1, transcendentals=0, bytes_accessed=1)
SWAP = [(0, 1), (1, 0)]
CORE = [(0, 1), (1, 0), (2, 3), (3, 2)]
YPAIR = [(0, 2), (2, 0), (1, 3), (3, 1)]
BUDDY = [(0, 1), (1, 0), (2, 3), (3, 2)]
PIECE = (0, 2, 1, 3)


def dot(a, b):
    return jnp.dot(a, b, preferred_element_type=F32)


def plain(
    ancestor, leaf_lower, leaf_upper, leaf_upper_inv, leaf_lower_inv, leaf_pivots, leaf_tiles,
    anc_upper_inv, anc_lower_inv, anc_pivots, anc_tiles, *, order,
):
    row_count, col_count = ancestor.shape
    panel_rows = leaf_upper.shape[2]
    width = leaf_lower.shape[-1]
    nt = leaf_tiles.shape[-1]
    tb = order // nt

    def onehot_tiles(first, count):
        tile = (first + jnp.arange(count, dtype=jnp.int32)) // tb
        return (tile[:, None] == jnp.arange(nt, dtype=jnp.int32)[None, :]).astype(F32)

    row_onehot = onehot_tiles(lax.axis_index("row") * row_count, row_count)
    col_onehot = onehot_tiles(lax.axis_index("col") * col_count, col_count)
    rows_all = lax.all_gather(leaf_upper[0], "row", axis=1, tiled=True)
    permuted = jnp.take_along_axis(rows_all, leaf_pivots[0][:, :, None], axis=1)
    upper_all = jnp.einsum("kij,kjc->kic", leaf_lower_inv[0], permuted, preferred_element_type=F32).astype(BF)
    own_lower = jnp.einsum("jrw,jwv->jrv", leaf_lower[0], leaf_upper_inv[0], preferred_element_type=F32).astype(BF)
    masks = jnp.einsum("rt,mts,cs->mrc", row_onehot, leaf_tiles[0].astype(F32), col_onehot)
    products = jnp.einsum(
        "mrw,mwc->mrc", lax.all_gather(own_lower, "col", axis=0, tiled=True), upper_all, preferred_element_type=F32
    )
    a_sum = ancestor + lax.psum(jnp.sum(masks * products, axis=0), "layer")
    gathered = lax.all_gather(a_sum[:panel_rows].astype(BF), "row", axis=0, tiled=True)
    anc_upper = dot(anc_lower_inv, jnp.take(gathered, anc_pivots, axis=0)).astype(BF)
    panel = dot(a_sum[:, :width].astype(BF), anc_upper_inv).astype(BF)
    kept = jnp.where(lax.axis_index("col") == 0, panel, 0).astype(BF)
    anc_lower = lax.psum(kept, "col")
    anc_mask = jnp.einsum("rt,ts,cs->rc", row_onehot, anc_tiles.astype(F32), col_onehot)
    return anc_lower, anc_upper, a_sum - anc_mask * dot(anc_lower, anc_upper)


def spec(shape, index=None):
    if index is None:
        return pl.BlockSpec(shape, lambda *_: (0,) * len(shape))
    return pl.BlockSpec(shape, index)


def step(body, name, place, operands, outs, *, in_specs=None, out_specs=None, grid=(1,)):
    in_specs = in_specs or [None] * len(operands)
    in_specs = [spec(o.shape) if i is None else i for o, i in zip(operands, in_specs)]
    out_specs = out_specs or [spec(o) for o in outs]
    made = pl.pallas_call(
        body,
        grid_spec=pltpu.PrefetchScalarGridSpec(
            num_scalar_prefetch=1, grid=grid, in_specs=in_specs, out_specs=out_specs
        ),
        out_shape=[jax.ShapeDtypeStruct(o, BF) for o in outs],
        cost_estimate=COST,
        compiler_params=pltpu.CompilerParams(vmem_limit_bytes=16 * MIB),
        name=name,
    )(place, *operands)
    return made if len(made) > 1 else made[0]


def ends(place):
    return (place[1] == 0) | (place[1] == 3)


def lower_kernel(place, low, inv, out):
    out[0] = dot(low[0, 0], inv[0, 0]).astype(BF)


def stack_kernel(place, first, kept, came, out):
    out[0] = first[...]

    @pl.when(ends(place))
    def _():
        out[1] = kept[...]

    @pl.when(jnp.logical_not(ends(place)))
    def _():
        out[1] = came[...]


def pair_kernel(place, one, two, out):
    out[0] = one[...]
    out[1] = two[...]


def cross_kernel(place, keep, recv, out):
    out[0] = (keep[0, 0] + recv[0, 0].astype(F32)).astype(BF)


def spread_kernel(place, keep, recv, came, to_a, to_b):
    def mine(b):
        return (keep[0, b] + recv[0, b].astype(F32) + came[b].astype(F32)).astype(BF)

    to_a[...] = mine(0)
    to_b[...] = mine(1)


def total_kernel(place, arrived, kept, came, out):
    @pl.when(ends(place))
    def _():
        out[...] = (arrived[...].astype(F32) + kept[...].astype(F32)).astype(BF)

    @pl.when(jnp.logical_not(ends(place)))
    def _():
        out[...] = (arrived[...].astype(F32) + came[...].astype(F32)).astype(BF)


def panel_kernel(place, anc, tq, inv, out):
    w = inv.shape[0]
    out[...] = dot((anc[...] + tq[:, :w].astype(F32)).astype(BF), inv[...]).astype(BF)


def choose_kernel(place, own, came, out, *, source):
    @pl.when(lax.rem(place[1], source) == 0)
    def _():
        out[...] = own[...]

    @pl.when(lax.rem(place[1], source) != 0)
    def _():
        out[...] = came[...]


def pivot_kernel(place, anc, tq, ty, tc, out):
    for layer, top in ((0, tq), (2, ty), (1, tc.at[0]), (3, tc.at[1])):

        @pl.when(place[2] == layer)
        def _():
            out[...] = (anc[...] + top[...].astype(F32)).astype(BF)


def panel_upper_kernel(place, m_own, m_other, own, other, out):
    out[...] = (dot(m_own[...], own[...]) + dot(m_other[...], other[...])).astype(BF)


def upper_kernel(mo_ref, mt_ref, so_ref, st_ref, out_ref):
    total = dot(mo_ref[0], so_ref[0, 0]) + dot(mt_ref[0], st_ref[0, 0])
    out_ref[0, 0] = total.astype(BF)


def make_upper(m_own, m_other, s_own, s_other):
    blocks, pair, half, cw = s_own.shape
    w = m_own.shape[1]
    m_spec = pl.BlockSpec((1, w, half), lambda k, b: (k, 0, 0))
    s_spec = pl.BlockSpec((1, 1, half, cw), lambda k, b: (b, k, 0, 0))
    return pl.pallas_call(
        upper_kernel,
        grid=(pair, blocks),
        in_specs=[m_spec, m_spec, s_spec, s_spec],
        out_specs=pl.BlockSpec((1, 1, w, cw), lambda k, b: (b, k, 0, 0)),
        out_shape=jax.ShapeDtypeStruct((blocks, pair, w, cw), BF),
        cost_estimate=COST,
        compiler_params=pltpu.CompilerParams(vmem_limit_bytes=16 * MIB),
        name="upper",
    )(m_own, m_other, s_own, s_other)


def product_kernel(place, tiles, low0, low1, up0, up1, keep, send, *, g, c, nt, rt, ct, tb, pair, tj):
    b, j = pl.program_id(0), pl.program_id(1)
    x, z, l = place[0], place[1], place[2]
    odd = lax.rem(z, 2)
    column = jnp.where(b == 0, jnp.where(odd == 0, jnp.where(z == 0, 1, 0), jnp.where(z == 1, 3, 2)),
                       jnp.where(z == 0, 0, jnp.where(z == 3, 3, 3 - z)))
    column = column * ct + c * tj + j
    for p, flip in enumerate(PIECE):
        i = jnp.bitwise_xor(l, flip)
        rows = pl.ds(pl.multiple_of(i * tb, tb), tb)
        total = None
        for t, (low, up) in enumerate(((low0, up0), (low1, up1))):
            for k in range(pair):
                leaf = (z - odd + t) * pair + k
                flag = tiles[(leaf * nt + x * rt + g * 4 + i) * nt + column]
                term = dot(low[0, k, rows, :] * flag.astype(F32).astype(BF), up[0, k])
                total = term if total is None else total + term
        if p < 2:
            keep[p, 0] = total
        else:
            send[p - 2, 0] = total.astype(BF)


def products(place, tiles, lows, up0, up1, *, g, c, nt, rt, ct, tb):
    blocks, pair, w, cw = up0.shape
    tj = cw // tb
    rows = 4 * tb
    up_spec = pl.BlockSpec((1, pair, w, tb), lambda b, j, *_: (b, 0, 0, j))
    out_spec = pl.BlockSpec((2, 1, tb, tb), lambda b, j, *_: (0, b, 0, j))
    shared, at = lows
    low_specs = [pl.BlockSpec((1, pair, rows, w), lambda b, j, *_, t=t: (t, 0, at, 0)) for t in range(2)]
    return pl.pallas_call(
        functools.partial(product_kernel, g=g, c=c, nt=nt, rt=rt, ct=ct, tb=tb, pair=pair, tj=tj),
        grid_spec=pltpu.PrefetchScalarGridSpec(
            num_scalar_prefetch=2,
            grid=(blocks, tj),
            in_specs=[
                *low_specs,
                up_spec,
                up_spec,
            ],
            out_specs=[out_spec, out_spec],
        ),
        out_shape=[
            jax.ShapeDtypeStruct((2, blocks, tb, cw), F32),
            jax.ShapeDtypeStruct((2, blocks, tb, cw), BF),
        ],
        cost_estimate=COST,
        compiler_params=pltpu.CompilerParams(vmem_limit_bytes=24 * MIB),
        name="products",
    )(place, tiles, shared, shared, up0, up1)


def final_kernel(place, tiles, *refs, g, c, nt, rt, ct, tb, tj, first, with_lower):
    anc, tq, ty, tc, au, pq, py, pc = refs[:8]
    outs = refs[8:] if first else refs[8 + (2 if with_lower else 1):]
    p = pl.program_id(0)
    x, z, l = place[0], place[1], place[2]
    flip = jnp.where(p == 0, 0, jnp.where(p == 1, 2, jnp.where(p == 2, 1, 3)))
    i = x * rt + g * 4 + jnp.bitwise_xor(l, flip)

    def work(total, panel):
        if with_lower:
            outs[1][...] = panel
        for j in range(tj):
            cols = slice(j * tb, (j + 1) * tb)
            base = anc[:, cols] + total[:, cols].astype(F32)
            flag = tiles[i * nt + z * ct + c * tj + j] != 0

            @pl.when(flag)
            def _():
                outs[0][:, cols] = base - dot(panel, au[:, cols])

            @pl.when(jnp.logical_not(flag))
            def _():
                outs[0][:, cols] = base

    for q, (t, v) in enumerate(((tq, pq), (ty, py), (tc.at[0], pc.at[0]), (tc.at[1], pc.at[1]))):

        @pl.when(p == q)
        def _():
            work(t[...], v[...])


def final(place, tiles, ancestor, total, au, panel, kept, *, g, c, nt, rt, ct, tb, with_lower):
    rows, cols = ancestor.shape
    tq, ty, tc = total
    pq, py, pc = panel
    cw, w = tq.shape[1], pq.shape[1]
    tj = cw // tb
    first = kept is None

    def whole(shape):
        return pl.BlockSpec(shape, lambda p, *_: (0,) * len(shape))

    def tile_row(p, place):
        flip = jnp.where(p == 0, 0, jnp.where(p == 1, 2, jnp.where(p == 2, 1, 3)))
        return g * 4 + jnp.bitwise_xor(place[2], flip)

    out_specs = [pl.BlockSpec((tb, cw), lambda p, place, *_: (tile_row(p, place), c))]
    out_shape = [jax.ShapeDtypeStruct((rows, cols), F32)]
    if with_lower:
        out_specs.append(pl.BlockSpec((tb, w), lambda p, place, *_: (tile_row(p, place), 0)))
        out_shape.append(jax.ShapeDtypeStruct((rows, w), BF))
    in_specs = [
        pl.BlockSpec((tb, cw), lambda p, place, *_: (tile_row(p, place), c)),
        whole(tq.shape), whole(ty.shape), whole(tc.shape), whole(au.shape),
        whole(pq.shape), whole(py.shape), whole(pc.shape),
    ]
    operands = [ancestor, tq, ty, tc, au, pq, py, pc]
    aliases = {}
    if not first:
        for n in range(len(out_shape)):
            aliases[2 + len(operands)] = n
            operands.append(kept[n])
            in_specs.append(pl.BlockSpec(memory_space=pl.ANY))
    return pl.pallas_call(
        functools.partial(
            final_kernel, g=g, c=c, nt=nt, rt=rt, ct=ct, tb=tb, tj=tj, first=first, with_lower=with_lower
        ),
        grid_spec=pltpu.PrefetchScalarGridSpec(
            num_scalar_prefetch=2, grid=(4,), in_specs=in_specs, out_specs=out_specs
        ),
        out_shape=out_shape,
        input_output_aliases=aliases,
        cost_estimate=COST,
        compiler_params=pltpu.CompilerParams(vmem_limit_bytes=24 * MIB),
        name="final",
    )(place, tiles, *operands)


def onehot_cols(inverse, pivots, first, count):
    wanted = (first + jnp.arange(count, dtype=jnp.int32))
    picks = (pivots[..., :, None] == wanted).astype(BF)
    return jnp.einsum("...it,...tj->...ij", inverse, picks, preferred_element_type=F32).astype(BF)


def after(value, *earlier):
    return lax.optimization_barrier((value, *earlier))[0]


def paired(
    ancestor, leaf_lower, leaf_upper, leaf_upper_inv, leaf_lower_inv, leaf_pivots, leaf_tiles,
    anc_upper_inv, anc_lower_inv, anc_pivots, anc_tiles, *, order, split,
):
    rows, cols = ancestor.shape
    pair, w = leaf_lower.shape[1], leaf_lower.shape[-1]
    half = leaf_upper.shape[2]
    nt = leaf_tiles.shape[-1]
    tb = order // nt
    rt, ct = rows // tb, cols // tb
    groups, cw = rows // (4 * tb), cols // split
    x, z, l = lax.axis_index("row"), lax.axis_index("col"), lax.axis_index("layer")
    odd = lax.rem(z, 2)
    is_end = (z == 0) | (z == 3)
    near, far = (z // 2) * 2 * pair, (1 - z // 2) * 2 * pair
    place = jnp.stack([x, z, l]).astype(jnp.int32)
    tiles = leaf_tiles.reshape(-1)
    top_tiles = anc_tiles.reshape(-1)
    shape = dict(nt=nt, rt=rt, ct=ct, tb=tb)
    u = leaf_upper[0]
    chunks = sorted(((g, c) for c in range(split) for g in range(groups)), key=lambda gc: (gc[0] + 1.5 * gc[1]))
    parts = [(c, t) for c in range(split) for t in range(2)]
    v = {}
    last = [place]

    def ordered(value):
        return after(value, last[0])

    def done(name, value, token=None):
        v[name] = value
        last[0] = value if token is None else token

    def slices(m):
        c, t = parts[m]
        src = ordered(u)

        def part(first):
            return lax.dynamic_slice(src, (first, 0, c * cw), (pair, half, cw))

        to_a = part(jnp.where(is_end, far, near) + t * pair)
        to_b = part(jnp.where(is_end, near, far) + t * pair)
        to_a, to_b = lax.optimization_barrier((to_a, to_b))
        v["a", m] = lax.ppermute(to_a, "col", [(1, 0), (2, 3), (0, 2), (3, 1)])
        v["b", m] = (to_b, lax.ppermute(to_b, "col", [(1, 2), (2, 1)]))
        last[0] = to_b

    def lower(first, count):
        n = count * 4
        own = step(
            lower_kernel, "lower", place, [ordered(leaf_lower), leaf_upper_inv], [(pair, n * tb, w)],
            in_specs=[
                spec((1, 1, tb, w), lambda k, i, *_: (0, k, first * 4 + i, 0)),
                spec((1, 1, w, w), lambda k, i, *_: (0, k, 0, 0)),
            ],
            out_specs=[spec((1, tb, w), lambda k, i, *_: (k, i, 0))], grid=(pair, n),
        )
        done(("lower", first), own)

    def share(first, count):
        own = v["lower", first]
        got = lax.all_gather(own, "col", axis_index_groups=[[0, 1], [2, 3]], axis=0, tiled=False)
        for g in range(first, first + count):
            v["low", g] = got, g - first

    def stack(m):
        kept, came = v["b", m]
        own = step(stack_kernel, "stack", place, [ordered(v["a", m]), kept, came], [(2, pair, half, cw)])
        done(("own", m), own)
        v["other", m] = lax.ppermute(own, "row", SWAP)

    def matrices():
        for t in range(2):
            first = near + t * pair
            inverse = ordered(lax.dynamic_slice_in_dim(leaf_lower_inv[0], first, pair, 0))
            pivots = lax.dynamic_slice_in_dim(leaf_pivots[0], first, pair, 0)
            one = onehot_cols(inverse, pivots, x * half, half)
            two = onehot_cols(inverse, pivots, (1 - x) * half, half)
            done(("m", t), (one, two), two)
        inverse = ordered(anc_lower_inv)
        one = onehot_cols(inverse, anc_pivots, x * half, half)
        two = onehot_cols(inverse, anc_pivots, (1 - x) * half, half)
        done("anc_m", (one, two), two)

    def upper(m):
        own = ordered(v["own", m])
        done(("upper",) + parts[m], make_upper(*v["m", parts[m][1]], own, v["other", m]))

    def multiply(n):
        g, c = chunks[n]
        keep, send = products(
            place, tiles, v["low", g], ordered(v["upper", c, 0]), v["upper", c, 1], g=g, c=c, **shape
        )
        done(("keep", n), keep, send)
        v["core", n] = lax.ppermute(send, "layer", CORE)

    def cross(n):
        crossing = step(
            cross_kernel, "cross", place, [ordered(v["keep", n]), v["core", n]], [(2, tb, cw)],
            in_specs=[spec((1, 1, tb, cw), lambda b, *_: (1, b, 0, 0))] * 2,
            out_specs=[spec((1, tb, cw), lambda b, *_: (b, 0, 0))], grid=(2,),
        )
        v["y", n] = lax.ppermute(crossing, "layer", YPAIR)
        last[0] = crossing

    def spread(n):
        to_a, to_b = step(
            spread_kernel, "spread", place, [ordered(v["keep", n]), v["core", n], v["y", n]], [(tb, cw)] * 2,
            in_specs=[spec((1, 2, tb, cw))] * 2 + [None],
        )
        v["qa", n] = lax.ppermute(to_a, "col", [(0, 1), (3, 2), (1, 3), (2, 0)])
        v["qb", n] = (to_b, lax.ppermute(to_b, "col", [(1, 2), (2, 1)]))
        last[0] = to_b

    def total(n):
        kept, came = v["qb", n]
        tq = step(total_kernel, "total", place, [ordered(v["qa", n]), kept, came], [(tb, cw)])
        v["ty", n] = lax.ppermute(tq, "layer", YPAIR)
        done(("tq", n), tq)

    def both(one, two):
        return step(pair_kernel, "pair", place, [ordered(one), two], [(2,) + one.shape])

    def gather(n):
        two = both(v["tq", n], v["ty", n])
        v["tc", n] = lax.ppermute(two, "layer", CORE)
        last[0] = two

    def panel(n):
        g, c = chunks[n]
        pq = step(
            panel_kernel, "panel", place, [ancestor, ordered(v["tq", n]), anc_upper_inv], [(tb, w)],
            in_specs=[spec((tb, w), lambda i, p: (g * 4 + p[2], 0)), None, None],
        )
        v["p1", g] = (pq, lax.ppermute(pq, "col", [(0, 2)]))
        last[0] = pq

    def choose(source, own, came):
        return step(
            functools.partial(choose_kernel, source=source), "choose", place, [ordered(own), came], [own.shape]
        )

    def panel_two(n):
        g, c = chunks[n]
        pq = choose(4, *v["p1", g])
        v["p2", g] = (pq, lax.ppermute(pq, "col", [(0, 1), (2, 3)]))
        last[0] = pq

    def panel_y(n):
        g, c = chunks[n]
        pq = choose(2, *v["p2", g])
        v["py", g] = lax.ppermute(pq, "layer", YPAIR)
        done(("pq", g), pq)

    def panel_core(n):
        g, c = chunks[n]
        two = both(v["pq", g], v["py", g])
        v["pc", g] = lax.ppermute(two, "layer", CORE)
        last[0] = two

    def pivot(n):
        g, c = chunks[n]
        rows_own = step(
            pivot_kernel, "pivot", place, [ancestor, ordered(v["tq", n]), v["ty", n], v["tc", n]], [(tb, cw)],
            in_specs=[spec((tb, cw), lambda *_: (0, c)), None, None, None],
        )
        v["pivot", c] = (rows_own, lax.ppermute(rows_own, "row", SWAP))
        last[0] = rows_own

    def pivot_two(n):
        g, c = chunks[n]
        one, two = v["anc_m"]
        rows_own, rows_other = v["pivot", c]
        done(("anc_upper", c), step(
            panel_upper_kernel, "anc_upper", place, [one, two, ordered(rows_own), rows_other], [(w, cw)]
        ))

    out = {}

    def finish(n):
        g, c = chunks[n]
        with_lower = c == 0
        kept = None if not out else ((out["schur"], out["lower"]) if with_lower else (out["schur"],))
        made = final(
            place, top_tiles, ancestor, (ordered(v["tq", n]), v["ty", n], v["tc", n]), v["anc_upper", c],
            (v["pq", g], v["py", g], v["pc", g]), kept, g=g, c=c, with_lower=with_lower, **shape,
        )
        out["schur"] = made[0]
        if with_lower:
            out["lower"] = made[1]
        last[0] = made[0]

    slices(0)
    lower(0, 1)
    slices(1)
    share(0, 1)
    slices(2)
    lower(1, groups - 1)
    slices(3)
    stack(0)
    matrices()
    stack(1)
    last[0] = after(last[0], v["low", 0][0])
    v["lower", 1] = after(v["lower", 1], last[0])
    share(1, groups - 1)
    upper(0)
    stack(2)
    upper(1)
    work = [(0, 3.5, stack, 3), (1, 1.5, upper, 2), (3, 1.5, upper, 3)]
    for n, (g, c) in enumerate(chunks):
        slot = n + GAP * (n > 0)
        steps = [
            (0, 0, multiply), (1, 1, spread), (2, 2, total), (0, 3, cross), (3, 4, gather),
        ]
        if g == 0:
            steps += [(3, 6, pivot), (4, 5, pivot_two)]
        if c == 0:
            steps += [(2, 2.1, panel), (3, 4.1, panel_two), (4, 4.2, panel_y), (5, 4.3, panel_core)]
        steps.append((5 if c == 0 else 4, 7, finish))
        work += [(slot + lag, position, stage, n) for lag, position, stage in steps]
    for _, _, stage, n in sorted(work, key=lambda e: e[:2]):
        stage(n)
    anc_upper = jnp.concatenate([v["anc_upper", c] for c in range(split)], axis=1)
    return out["lower"], anc_upper, out["schur"]


def solution(mesh):
    sizes = mesh.shape

    def shards(*args):
        ancestor, leaf_lower, leaf_upper, leaf_tiles = args[0], args[1], args[2], args[6]
        rows, cols = ancestor.shape
        order = rows * sizes["row"]
        nt = leaf_tiles.shape[-1]
        tb = order // nt
        w, half = leaf_lower.shape[-1], leaf_upper.shape[2]
        fits = (
            (sizes["layer"], sizes["row"], sizes["col"]) == (4, 2, 4)
            and leaf_lower.shape[0] == 1 and leaf_upper.shape[1] == 4 * leaf_lower.shape[1]
            and order % nt == 0 and rows % (4 * tb) == 0 and cols % (2 * tb) == 0
            and half == tb and tb % 128 == 0 and w <= cols // 2
        )
        if fits:
            return paired(*args, order=order, split=2)
        return plain(*args, order=order)

    return jax.shard_map(
        shards,
        mesh=mesh,
        in_specs=(
            P("row", "col"), P("layer", "col", "row", None), P("layer", None, "row", "col"),
            P("layer", "col", None, None), P("layer", None, None, None), P("layer", None, None),
            P("layer", None, None, None), P(), P(), P(), P(),
        ),
        out_specs=(P("row", None), P(None, "col"), P("row", "col")),
        check_vma=False,
    )
```

```python
import functools

import jax
import jax.numpy as jnp
from jax import lax
from jax.experimental import pallas as pl
from jax.experimental.pallas import tpu as pltpu
from jax.sharding import PartitionSpec as P

BF = jnp.bfloat16
F32 = jnp.float32
MIB = 1024 * 1024
GAP = 2
SMALL, MAIN, WIDE = 16 * MIB, 20 * MIB, 48 * MIB
COST = pl.CostEstimate(flops=1, transcendentals=0, bytes_accessed=1)
LONG = pl.CostEstimate(flops=5 * 10**13, transcendentals=0, bytes_accessed=1)
SWAP = [(0, 1), (1, 0)]
CORE = [(0, 1), (1, 0), (2, 3), (3, 2)]
YPAIR = [(0, 2), (2, 0), (1, 3), (3, 1)]
BUDDY = [(0, 1), (1, 0), (2, 3), (3, 2)]
PIECE = (0, 2, 1, 3)


def dot(a, b):
    return jnp.dot(a, b, preferred_element_type=F32)


def plain(
    ancestor, leaf_lower, leaf_upper, leaf_upper_inv, leaf_lower_inv, leaf_pivots, leaf_tiles,
    anc_upper_inv, anc_lower_inv, anc_pivots, anc_tiles, *, order,
):
    row_count, col_count = ancestor.shape
    panel_rows = leaf_upper.shape[2]
    width = leaf_lower.shape[-1]
    nt = leaf_tiles.shape[-1]
    tb = order // nt

    def onehot_tiles(first, count):
        tile = (first + jnp.arange(count, dtype=jnp.int32)) // tb
        return (tile[:, None] == jnp.arange(nt, dtype=jnp.int32)[None, :]).astype(F32)

    row_onehot = onehot_tiles(lax.axis_index("row") * row_count, row_count)
    col_onehot = onehot_tiles(lax.axis_index("col") * col_count, col_count)
    rows_all = lax.all_gather(leaf_upper[0], "row", axis=1, tiled=True)
    permuted = jnp.take_along_axis(rows_all, leaf_pivots[0][:, :, None], axis=1)
    upper_all = jnp.einsum("kij,kjc->kic", leaf_lower_inv[0], permuted, preferred_element_type=F32).astype(BF)
    own_lower = jnp.einsum("jrw,jwv->jrv", leaf_lower[0], leaf_upper_inv[0], preferred_element_type=F32).astype(BF)
    masks = jnp.einsum("rt,mts,cs->mrc", row_onehot, leaf_tiles[0].astype(F32), col_onehot)
    products = jnp.einsum(
        "mrw,mwc->mrc", lax.all_gather(own_lower, "col", axis=0, tiled=True), upper_all, preferred_element_type=F32
    )
    a_sum = ancestor + lax.psum(jnp.sum(masks * products, axis=0), "layer")
    gathered = lax.all_gather(a_sum[:panel_rows].astype(BF), "row", axis=0, tiled=True)
    anc_upper = dot(anc_lower_inv, jnp.take(gathered, anc_pivots, axis=0)).astype(BF)
    panel = dot(a_sum[:, :width].astype(BF), anc_upper_inv).astype(BF)
    kept = jnp.where(lax.axis_index("col") == 0, panel, 0).astype(BF)
    anc_lower = lax.psum(kept, "col")
    anc_mask = jnp.einsum("rt,ts,cs->rc", row_onehot, anc_tiles.astype(F32), col_onehot)
    return anc_lower, anc_upper, a_sum - anc_mask * dot(anc_lower, anc_upper)


def spec(shape, index=None):
    if index is None:
        return pl.BlockSpec(shape, lambda *_: (0,) * len(shape))
    return pl.BlockSpec(shape, index)


def step(body, name, place, operands, outs, *, in_specs=None, out_specs=None, grid=(1,), cost=COST, vmem=SMALL):
    in_specs = in_specs or [None] * len(operands)
    in_specs = [spec(o.shape) if i is None else i for o, i in zip(operands, in_specs)]
    out_specs = out_specs or [spec(o) for o in outs]
    made = pl.pallas_call(
        body,
        grid_spec=pltpu.PrefetchScalarGridSpec(
            num_scalar_prefetch=1, grid=grid, in_specs=in_specs, out_specs=out_specs
        ),
        out_shape=[jax.ShapeDtypeStruct(o, BF) for o in outs],
        cost_estimate=cost,
        compiler_params=pltpu.CompilerParams(vmem_limit_bytes=vmem),
        name=name,
    )(place, *operands)
    return made if len(made) > 1 else made[0]


def ends(place):
    return (place[1] == 0) | (place[1] == 3)


def copy_kernel(place, one, two, to_a, to_b):
    to_a[...] = one[0]
    to_b[...] = two[0]


def matrix_kernel(place, inv, pivots, out):
    half = out.shape[-1]
    for side in range(2):
        first = jnp.bitwise_xor(place[0], side) * half
        wanted = first + lax.broadcasted_iota(jnp.int32, (half, inv.shape[-1]), 0)
        picks = (wanted == pivots[...].reshape(1, -1)).astype(F32).astype(BF)
        product = lax.dot_general(
            inv[...].reshape(inv.shape[-2:]), picks, (((1,), (1,)), ((), ())), preferred_element_type=F32
        )
        out[side, ...] = product.astype(BF).reshape(out.shape[1:])


def lower_kernel(place, low, inv, out):
    out[0] = dot(low[0, 0], inv[0, 0]).astype(BF)


def stack_kernel(place, first, kept, came, out):
    out[0] = first[...]

    @pl.when(ends(place))
    def _():
        out[1] = kept[...]

    @pl.when(jnp.logical_not(ends(place)))
    def _():
        out[1] = came[...]


def pair_kernel(place, one, two, out):
    out[0] = one[...]
    out[1] = two[...]


def cross_kernel(place, keep, recv, out):
    out[0] = (keep[0, 0] + recv[0, 0].astype(F32)).astype(BF)


def spread_kernel(place, keep, recv, came, to_a, to_b):
    def mine(b):
        return (keep[0, b] + recv[0, b].astype(F32) + came[b].astype(F32)).astype(BF)

    to_a[...] = mine(0)
    to_b[...] = mine(1)


def total_kernel(place, arrived, kept, came, out):
    @pl.when(ends(place))
    def _():
        out[...] = (arrived[...].astype(F32) + kept[...].astype(F32)).astype(BF)

    @pl.when(jnp.logical_not(ends(place)))
    def _():
        out[...] = (arrived[...].astype(F32) + came[...].astype(F32)).astype(BF)


def panel_kernel(place, anc, tq, inv, out):
    w = inv.shape[0]
    out[...] = dot((anc[...] + tq[:, :w].astype(F32)).astype(BF), inv[...]).astype(BF)


def choose_kernel(place, own, came, out, *, source):
    @pl.when(lax.rem(place[1], source) == 0)
    def _():
        out[...] = own[...]

    @pl.when(lax.rem(place[1], source) != 0)
    def _():
        out[...] = came[...]


def pivot_kernel(place, anc, tq, ty, tc, out):
    for layer, top in ((0, tq), (2, ty), (1, tc.at[0]), (3, tc.at[1])):

        @pl.when(place[2] == layer)
        def _():
            out[...] = (anc[...] + top[...].astype(F32)).astype(BF)


def panel_upper_kernel(place, m, own, other, out):
    out[...] = (dot(m[0], own[...]) + dot(m[1], other[...])).astype(BF)


def upper_kernel(mo_ref, mt_ref, so_ref, st_ref, out_ref):
    total = dot(mo_ref[0, 0], so_ref[0, 0]) + dot(mt_ref[0, 0], st_ref[0, 0])
    out_ref[0, 0] = total.astype(BF)


def make_upper(m_own, m_other, s_own, s_other):
    blocks, pair, half, cw = s_own.shape
    w = m_own.shape[2]
    m_specs = [pl.BlockSpec((1, 1, w, half), lambda k, b, side=side: (side, k, 0, 0)) for side in range(2)]
    s_spec = pl.BlockSpec((1, 1, half, cw), lambda k, b: (b, k, 0, 0))
    return pl.pallas_call(
        upper_kernel,
        grid=(pair, blocks),
        in_specs=[*m_specs, s_spec, s_spec],
        out_specs=pl.BlockSpec((1, 1, w, cw), lambda k, b: (b, k, 0, 0)),
        out_shape=jax.ShapeDtypeStruct((blocks, pair, w, cw), BF),
        cost_estimate=COST,
        compiler_params=pltpu.CompilerParams(vmem_limit_bytes=SMALL),
        name="upper",
    )(m_own, m_other, s_own, s_other)


def product_kernel(place, tiles, low0, low1, up0, up1, keep, send, *, swapped, g, c, nt, rt, ct, tb, pair, tj):
    b, j = pl.program_id(0), pl.program_id(1)
    x, z, l = place[0], place[1], place[2]
    odd = lax.rem(z, 2)
    column = jnp.where(b == 0, jnp.where(odd == 0, jnp.where(z == 0, 1, 0), jnp.where(z == 1, 3, 2)),
                       jnp.where(z == 0, 0, jnp.where(z == 3, 3, 3 - z)))
    column = column * ct + c * tj + j
    for p, flip in enumerate(PIECE):
        i = jnp.bitwise_xor(l, flip)
        rows = pl.ds(pl.multiple_of(i * tb, tb), tb)
        total = None
        for t, low in enumerate((low0, low1)):
            owner = jnp.bitwise_xor(z, t) if swapped else z - odd + t
            for k in range(pair):
                flag = tiles[((owner * pair + k) * nt + x * rt + g * 4 + i) * nt + column]
                left = low[0, k, rows, :] * flag.astype(F32).astype(BF)
                if swapped:
                    right = jnp.where(odd == t, up0[0, k], up1[0, k])
                else:
                    right = (up0, up1)[t][0, k]
                term = dot(left, right)
                total = term if total is None else total + term
        if p < 2:
            keep[p, 0] = total
        else:
            send[p - 2, 0] = total.astype(BF)


def products(place, tiles, lows, up0, up1, *, g, c, nt, rt, ct, tb):
    blocks, pair, w, cw = up0.shape
    tj = cw // tb
    rows = 4 * tb
    up_spec = pl.BlockSpec((1, pair, w, tb), lambda b, j, *_: (b, 0, 0, j))
    out_spec = pl.BlockSpec((2, 1, tb, tb), lambda b, j, *_: (0, b, 0, j))
    one, two, at, swapped = lows
    low_specs = [pl.BlockSpec((1, pair, rows, w), lambda b, j, *_, t=t: (t, 0, at, 0)) for t in (one[1], two[1])]
    return pl.pallas_call(
        functools.partial(product_kernel, swapped=swapped, g=g, c=c, nt=nt, rt=rt, ct=ct, tb=tb, pair=pair, tj=tj),
        grid_spec=pltpu.PrefetchScalarGridSpec(
            num_scalar_prefetch=2,
            grid=(blocks, tj),
            in_specs=[
                *low_specs,
                up_spec,
                up_spec,
            ],
            out_specs=[out_spec, out_spec],
        ),
        out_shape=[
            jax.ShapeDtypeStruct((2, blocks, tb, cw), F32),
            jax.ShapeDtypeStruct((2, blocks, tb, cw), BF),
        ],
        cost_estimate=COST,
        compiler_params=pltpu.CompilerParams(vmem_limit_bytes=MAIN),
        name="products",
    )(place, tiles, one[0], two[0], up0, up1)


def final_kernel(place, tiles, *refs, g, c, nt, rt, ct, tb, tj, first, with_lower):
    anc, tq, ty, tc, au, pq, py, pc = refs[:8]
    outs = refs[8:] if first else refs[8 + (2 if with_lower else 1):]
    p = pl.program_id(0)
    x, z, l = place[0], place[1], place[2]
    flip = jnp.where(p == 0, 0, jnp.where(p == 1, 2, jnp.where(p == 2, 1, 3)))
    i = x * rt + g * 4 + jnp.bitwise_xor(l, flip)

    def work(total, panel):
        if with_lower:
            outs[1][...] = panel
        for j in range(tj):
            cols = slice(j * tb, (j + 1) * tb)
            base = anc[:, cols] + total[:, cols].astype(F32)
            flag = tiles[i * nt + z * ct + c * tj + j] != 0

            @pl.when(flag)
            def _():
                outs[0][:, cols] = base - dot(panel, au[:, cols])

            @pl.when(jnp.logical_not(flag))
            def _():
                outs[0][:, cols] = base

    for q, (t, v) in enumerate(((tq, pq), (ty, py), (tc.at[0], pc.at[0]), (tc.at[1], pc.at[1]))):

        @pl.when(p == q)
        def _():
            work(t[...], v[...])


def final(place, tiles, ancestor, total, au, panel, kept, *, g, c, nt, rt, ct, tb, with_lower):
    rows, cols = ancestor.shape
    tq, ty, tc = total
    pq, py, pc = panel
    cw, w = tq.shape[1], pq.shape[1]
    tj = cw // tb
    first = kept is None

    def whole(shape):
        return pl.BlockSpec(shape, lambda p, *_: (0,) * len(shape))

    def tile_row(p, place):
        flip = jnp.where(p == 0, 0, jnp.where(p == 1, 2, jnp.where(p == 2, 1, 3)))
        return g * 4 + jnp.bitwise_xor(place[2], flip)

    out_specs = [pl.BlockSpec((tb, cw), lambda p, place, *_: (tile_row(p, place), c))]
    out_shape = [jax.ShapeDtypeStruct((rows, cols), F32)]
    if with_lower:
        out_specs.append(pl.BlockSpec((tb, w), lambda p, place, *_: (tile_row(p, place), 0)))
        out_shape.append(jax.ShapeDtypeStruct((rows, w), BF))
    in_specs = [
        pl.BlockSpec((tb, cw), lambda p, place, *_: (tile_row(p, place), c)),
        whole(tq.shape), whole(ty.shape), whole(tc.shape), whole(au.shape),
        whole(pq.shape), whole(py.shape), whole(pc.shape),
    ]
    operands = [ancestor, tq, ty, tc, au, pq, py, pc]
    aliases = {}
    if not first:
        for n in range(len(out_shape)):
            aliases[2 + len(operands)] = n
            operands.append(kept[n])
            in_specs.append(pl.BlockSpec(memory_space=pl.ANY))
    return pl.pallas_call(
        functools.partial(
            final_kernel, g=g, c=c, nt=nt, rt=rt, ct=ct, tb=tb, tj=tj, first=first, with_lower=with_lower
        ),
        grid_spec=pltpu.PrefetchScalarGridSpec(
            num_scalar_prefetch=2, grid=(4,), in_specs=in_specs, out_specs=out_specs
        ),
        out_shape=out_shape,
        input_output_aliases=aliases,
        cost_estimate=COST,
        compiler_params=pltpu.CompilerParams(vmem_limit_bytes=WIDE),
        name="final",
    )(place, tiles, *operands)


def after(value, *earlier):
    return lax.optimization_barrier((value, *earlier))[0]


def paired(
    ancestor, leaf_lower, leaf_upper, leaf_upper_inv, leaf_lower_inv, leaf_pivots, leaf_tiles,
    anc_upper_inv, anc_lower_inv, anc_pivots, anc_tiles, *, order, split,
):
    rows, cols = ancestor.shape
    pair, w = leaf_lower.shape[1], leaf_lower.shape[-1]
    half = leaf_upper.shape[2]
    nt = leaf_tiles.shape[-1]
    tb = order // nt
    rt, ct = rows // tb, cols // tb
    groups, cw = rows // (4 * tb), cols // split
    x, z, l = lax.axis_index("row"), lax.axis_index("col"), lax.axis_index("layer")
    odd = lax.rem(z, 2)
    is_end = (z == 0) | (z == 3)
    near, far = (z // 2) * 2 * pair, (1 - z // 2) * 2 * pair
    place = jnp.stack([x, z, l]).astype(jnp.int32)
    tiles = leaf_tiles.reshape(-1)
    top_tiles = anc_tiles.reshape(-1)
    shape = dict(nt=nt, rt=rt, ct=ct, tb=tb)
    u = leaf_upper[0]
    chunks = sorted(((g, c) for c in range(split) for g in range(groups)), key=lambda gc: (gc[0] > 0, gc[1] * 1.5 + gc[0], gc[0]))
    parts = [(c, t) for c in range(split) for t in range(2)]
    v = {}
    last = [place]

    def ordered(value):
        return after(value, last[0])

    def done(name, value, token=None):
        v[name] = value
        last[0] = value if token is None else token

    def slices(m):
        c, t = parts[m]

        def near_pair(p):
            return p[1] // 2 * 2

        def far_pair(p):
            return 2 - p[1] // 2 * 2

        def one(k, p):
            return (0, jnp.where(ends(p), far_pair(p), near_pair(p)) + t, k, 0, c)

        def two(k, p):
            return (0, jnp.where(ends(p), near_pair(p), far_pair(p)) + t, k, 0, c)

        src = ordered(leaf_upper)
        src = src.reshape((1, src.shape[1] // pair, pair) + src.shape[2:])
        block = (1, 1, 1, half, cw)
        to_a, to_b = step(
            lambda place, i, j, o, q: copy_kernel(place, i.at[0, 0], j.at[0, 0], o.at[0], q.at[0]), "slices", place,
            [src, src], [(pair, half, cw)] * 2, in_specs=[spec(block, one), spec(block, two)],
            out_specs=[spec((1, half, cw), lambda k, p: (k, 0, 0))] * 2, grid=(pair,), vmem=WIDE,
        )
        v["a", m] = lax.ppermute(to_a, "col", [(1, 0), (2, 3), (0, 2), (3, 1)])
        v["b", m] = (to_b, lax.ppermute(to_b, "col", [(1, 2), (2, 1)]))
        last[0] = to_b

    def lower(first, count):
        n = count * 4
        own = step(
            lower_kernel, "lower", place, [ordered(leaf_lower), leaf_upper_inv], [(pair, n * tb, w)],
            in_specs=[
                spec((1, 1, tb, w), lambda k, i, *_: (0, k, first * 4 + i, 0)),
                spec((1, 1, w, w), lambda k, i, *_: (0, k, 0, 0)),
            ],
            out_specs=[spec((1, tb, w), lambda k, i, *_: (k, i, 0))], grid=(pair, n),
        )
        done(("lower", first), own)

    def share(first, count):
        own = v["lower", first]
        got = lax.all_gather(own, "col", axis_index_groups=[[0, 1], [2, 3]], axis=0, tiled=False)
        for g in range(first, first + count):
            v["low", g] = (got, 0), (got, 1), g - first, False

    def exchange(g):
        own = v["lower", g][None]
        v["low", g] = (own, 0), (lax.ppermute(own, "col", BUDDY), 0), 0, True

    def stack(m):
        kept, came = v["b", m]
        own = step(stack_kernel, "stack", place, [ordered(v["a", m]), kept, came], [(2, pair, half, cw)])
        done(("own", m), own)
        v["other", m] = lax.ppermute(own, "row", SWAP)

    def matrices():
        pivots = leaf_pivots.reshape(leaf_pivots.shape[1], 1, w)
        for t in range(2):
            both = step(
                matrix_kernel, "matrix", place, [ordered(leaf_lower_inv), pivots], [(2, pair, w, half)],
                in_specs=[
                    spec((1, 1, w, w), lambda k, p: (0, p[1] // 2 * 2 * pair + t * pair + k, 0, 0)),
                    spec((1, 1, w), lambda k, p: (p[1] // 2 * 2 * pair + t * pair + k, 0, 0)),
                ],
                out_specs=[spec((2, 1, w, half), lambda k, p: (0, k, 0, 0))], grid=(pair,), vmem=WIDE,
            )
            done(("m", t), (both, both), both)
        both = step(
            matrix_kernel, "matrix", place, [ordered(anc_lower_inv), anc_pivots.reshape(1, w)], [(2, w, half)],
        )
        done("anc_m", both, both)

    def upper(m):
        own = ordered(v["own", m])
        done(("upper",) + parts[m], make_upper(*v["m", parts[m][1]], own, v["other", m]))

    def multiply(n):
        g, c = chunks[n]
        keep, send = products(
            place, tiles, v["low", g], ordered(v["upper", c, 0]), v["upper", c, 1], g=g, c=c, **shape
        )
        done(("keep", n), keep, send)
        v["core", n] = lax.ppermute(send, "layer", CORE)

    def cross(n):
        crossing = step(
            cross_kernel, "cross", place, [ordered(v["keep", n]), v["core", n]], [(2, tb, cw)],
            in_specs=[spec((1, 1, tb, cw), lambda b, *_: (1, b, 0, 0))] * 2,
            out_specs=[spec((1, tb, cw), lambda b, *_: (b, 0, 0))], grid=(2,),
        )
        v["y", n] = lax.ppermute(crossing, "layer", YPAIR)
        last[0] = crossing

    def spread(n):
        to_a, to_b = step(
            spread_kernel, "spread", place, [ordered(v["keep", n]), v["core", n], v["y", n]], [(tb, cw)] * 2,
            in_specs=[spec((1, 2, tb, cw))] * 2 + [None], cost=LONG if n else COST,
        )
        v["qa", n] = lax.ppermute(to_a, "col", [(0, 1), (3, 2), (1, 3), (2, 0)])
        v["qb", n] = (to_b, lax.ppermute(to_b, "col", [(1, 2), (2, 1)]))
        last[0] = to_b

    def total(n):
        kept, came = v["qb", n]
        tq = step(total_kernel, "total", place, [ordered(v["qa", n]), kept, came], [(tb, cw)])
        v["ty", n] = lax.ppermute(tq, "layer", YPAIR)
        done(("tq", n), tq)

    def both(one, two):
        return step(pair_kernel, "pair", place, [ordered(one), two], [(2,) + one.shape])

    def gather(n):
        two = both(v["tq", n], v["ty", n])
        v["tc", n] = lax.ppermute(two, "layer", CORE)
        last[0] = two

    def panel(n):
        g, c = chunks[n]
        pq = step(
            panel_kernel, "panel", place, [ancestor, ordered(v["tq", n]), anc_upper_inv], [(tb, w)],
            in_specs=[spec((tb, w), lambda i, p: (g * 4 + p[2], 0)), None, None], vmem=WIDE,
        )
        v["p1", g] = (pq, lax.ppermute(pq, "col", [(0, 2)]))
        last[0] = pq

    def choose(source, own, came):
        return step(
            functools.partial(choose_kernel, source=source), "choose", place, [ordered(own), came], [own.shape]
        )

    def panel_two(n):
        g, c = chunks[n]
        pq = choose(4, *v["p1", g])
        v["p2", g] = (pq, lax.ppermute(pq, "col", [(0, 1), (2, 3)]))
        last[0] = pq

    def panel_y(n):
        g, c = chunks[n]
        pq = choose(2, *v["p2", g])
        v["py", g] = lax.ppermute(pq, "layer", YPAIR)
        done(("pq", g), pq)

    def panel_core(n):
        g, c = chunks[n]
        two = both(v["pq", g], v["py", g])
        v["pc", g] = lax.ppermute(two, "layer", CORE)
        last[0] = two

    def pivot(n):
        g, c = chunks[n]
        rows_own = step(
            pivot_kernel, "pivot", place, [ancestor, ordered(v["tq", n]), v["ty", n], v["tc", n]], [(tb, cw)],
            in_specs=[spec((tb, cw), lambda *_: (0, c)), None, None, None], vmem=WIDE,
        )
        v["pivot", c] = (rows_own, lax.ppermute(rows_own, "row", SWAP))
        last[0] = rows_own

    def pivot_two(n):
        g, c = chunks[n]
        rows_own, rows_other = v["pivot", c]
        done(("anc_upper", c), step(
            panel_upper_kernel, "anc_upper", place, [v["anc_m"], ordered(rows_own), rows_other], [(w, cw)]
        ))

    out = {}

    def finish(n):
        g, c = chunks[n]
        with_lower = c == 0
        kept = None if not out else ((out["schur"], out["lower"]) if with_lower else (out["schur"],))
        made = final(
            place, top_tiles, ancestor, (ordered(v["tq", n]), v["ty", n], v["tc", n]), v["anc_upper", c],
            (v["pq", g], v["py", g], v["pc", g]), kept, g=g, c=c, with_lower=with_lower, **shape,
        )
        out["schur"] = made[0]
        if with_lower:
            out["lower"] = made[1]
        last[0] = made[0]

    slices(0)
    slices(1)
    lower(0, 1)
    share(0, 1)
    slices(2)
    slices(3)
    lower(1, groups - 1)
    matrices()
    stack(0)
    stack(1)
    upper(0)
    last[0] = after(last[0], v["low", 0][0][0])
    v["lower", 1] = after(v["lower", 1], last[0])
    share(1, groups - 1)
    stack(2)
    upper(1)
    work = [(0, 3.5, stack, 3), (1, 1.5, upper, 2), (2, 6.5, upper, 3)]
    for n, (g, c) in enumerate(chunks):
        slot = n + GAP * (n > 0)
        steps = [(0, 0, multiply), (2, 2, total), (1, 2.9, spread), (0, 3, cross), (3, 4, gather)]
        if g == 0:
            steps += [(3, 6, pivot), (4, 5, pivot_two)]
        if c == 0:
            steps += [(2, 2.1, panel), (3, 4.1, panel_two), (4, 4.2, panel_y), (5, 4.3, panel_core)]
        steps.append((5 if c == 0 else 4, 7, finish))
        work += [(slot + lag, position, stage, n) for lag, position, stage in steps]
    for _, _, stage, n in sorted(work, key=lambda e: e[:2]):
        stage(n)
    anc_upper = jnp.concatenate([v["anc_upper", c] for c in range(split)], axis=1)
    return out["lower"], anc_upper, out["schur"]


def solution(mesh):
    sizes = mesh.shape

    def shards(*args):
        ancestor, leaf_lower, leaf_upper, leaf_tiles = args[0], args[1], args[2], args[6]
        rows, cols = ancestor.shape
        order = rows * sizes["row"]
        nt = leaf_tiles.shape[-1]
        tb = order // nt
        w, half = leaf_lower.shape[-1], leaf_upper.shape[2]
        fits = (
            (sizes["layer"], sizes["row"], sizes["col"]) == (4, 2, 4)
            and leaf_lower.shape[0] == 1 and leaf_upper.shape[1] == 4 * leaf_lower.shape[1]
            and order % nt == 0 and rows % (4 * tb) == 0 and cols % (2 * tb) == 0
            and half == tb and tb % 128 == 0 and w <= cols // 2
        )
        if fits:
            return paired(*args, order=order, split=2)
        return plain(*args, order=order)

    return jax.shard_map(
        shards,
        mesh=mesh,
        in_specs=(
            P("row", "col"), P("layer", "col", "row", None), P("layer", None, "row", "col"),
            P("layer", "col", None, None), P("layer", None, None, None), P("layer", None, None),
            P("layer", None, None, None), P(), P(), P(), P(),
        ),
        out_specs=(P("row", None), P(None, "col"), P("row", "col")),
        check_vma=False,
    )
```

```python
import functools

import jax
import jax.numpy as jnp
from jax import lax
from jax.experimental import pallas as pl
from jax.experimental.pallas import tpu as pltpu
from jax.sharding import PartitionSpec as P

BF = jnp.bfloat16
F32 = jnp.float32
MIB = 1024 * 1024
GAP = 2
SMALL, MAIN, WIDE = 16 * MIB, 20 * MIB, 48 * MIB
COST = pl.CostEstimate(flops=1, transcendentals=0, bytes_accessed=1)
LONG = pl.CostEstimate(flops=5 * 10**13, transcendentals=0, bytes_accessed=1)
SWAP = [(0, 1), (1, 0)]
CORE = [(0, 1), (1, 0), (2, 3), (3, 2)]
YPAIR = [(0, 2), (2, 0), (1, 3), (3, 1)]
BUDDY = [(0, 1), (1, 0), (2, 3), (3, 2)]
PIECE = (0, 2, 1, 3)


def dot(a, b):
    return jnp.dot(a, b, preferred_element_type=F32)


def plain(
    ancestor, leaf_lower, leaf_upper, leaf_upper_inv, leaf_lower_inv, leaf_pivots, leaf_tiles,
    anc_upper_inv, anc_lower_inv, anc_pivots, anc_tiles, *, order,
):
    row_count, col_count = ancestor.shape
    panel_rows = leaf_upper.shape[2]
    width = leaf_lower.shape[-1]
    nt = leaf_tiles.shape[-1]
    tb = order // nt

    def onehot_tiles(first, count):
        tile = (first + jnp.arange(count, dtype=jnp.int32)) // tb
        return (tile[:, None] == jnp.arange(nt, dtype=jnp.int32)[None, :]).astype(F32)

    row_onehot = onehot_tiles(lax.axis_index("row") * row_count, row_count)
    col_onehot = onehot_tiles(lax.axis_index("col") * col_count, col_count)
    rows_all = lax.all_gather(leaf_upper[0], "row", axis=1, tiled=True)
    permuted = jnp.take_along_axis(rows_all, leaf_pivots[0][:, :, None], axis=1)
    upper_all = jnp.einsum("kij,kjc->kic", leaf_lower_inv[0], permuted, preferred_element_type=F32).astype(BF)
    own_lower = jnp.einsum("jrw,jwv->jrv", leaf_lower[0], leaf_upper_inv[0], preferred_element_type=F32).astype(BF)
    masks = jnp.einsum("rt,mts,cs->mrc", row_onehot, leaf_tiles[0].astype(F32), col_onehot)
    products = jnp.einsum(
        "mrw,mwc->mrc", lax.all_gather(own_lower, "col", axis=0, tiled=True), upper_all, preferred_element_type=F32
    )
    a_sum = ancestor + lax.psum(jnp.sum(masks * products, axis=0), "layer")
    gathered = lax.all_gather(a_sum[:panel_rows].astype(BF), "row", axis=0, tiled=True)
    anc_upper = dot(anc_lower_inv, jnp.take(gathered, anc_pivots, axis=0)).astype(BF)
    panel = dot(a_sum[:, :width].astype(BF), anc_upper_inv).astype(BF)
    kept = jnp.where(lax.axis_index("col") == 0, panel, 0).astype(BF)
    anc_lower = lax.psum(kept, "col")
    anc_mask = jnp.einsum("rt,ts,cs->rc", row_onehot, anc_tiles.astype(F32), col_onehot)
    return anc_lower, anc_upper, a_sum - anc_mask * dot(anc_lower, anc_upper)


def spec(shape, index=None):
    if index is None:
        return pl.BlockSpec(shape, lambda *_: (0,) * len(shape))
    return pl.BlockSpec(shape, index)


def step(body, name, place, operands, outs, *, in_specs=None, out_specs=None, grid=(1,), cost=COST, vmem=SMALL):
    in_specs = in_specs or [None] * len(operands)
    in_specs = [spec(o.shape) if i is None else i for o, i in zip(operands, in_specs)]
    out_specs = out_specs or [spec(o) for o in outs]
    made = pl.pallas_call(
        body,
        grid_spec=pltpu.PrefetchScalarGridSpec(
            num_scalar_prefetch=1, grid=grid, in_specs=in_specs, out_specs=out_specs
        ),
        out_shape=[jax.ShapeDtypeStruct(o, BF) for o in outs],
        cost_estimate=cost,
        compiler_params=pltpu.CompilerParams(vmem_limit_bytes=vmem),
        name=name,
    )(place, *operands)
    return made if len(made) > 1 else made[0]


def ends(place):
    return (place[1] == 0) | (place[1] == 3)


def copy_kernel(place, one, two, to_a, to_b):
    to_a[...] = one[0]
    to_b[...] = two[0]


def matrix_kernel(place, inv, pivots, out):
    half = out.shape[-1]
    for side in range(2):
        first = jnp.bitwise_xor(place[0], side) * half
        wanted = first + lax.broadcasted_iota(jnp.int32, (half, inv.shape[-1]), 0)
        picks = (wanted == pivots[...].reshape(1, -1)).astype(F32).astype(BF)
        product = lax.dot_general(
            inv[...].reshape(inv.shape[-2:]), picks, (((1,), (1,)), ((), ())), preferred_element_type=F32
        )
        out[side, ...] = product.astype(BF).reshape(out.shape[1:])


def lower_kernel(place, low, inv, out):
    out[0] = dot(low[0, 0], inv[0, 0]).astype(BF)


def stack_kernel(place, first, kept, came, out):
    out[0] = first[...]

    @pl.when(ends(place))
    def _():
        out[1] = kept[...]

    @pl.when(jnp.logical_not(ends(place)))
    def _():
        out[1] = came[...]


def pair_kernel(place, one, two, out):
    out[0] = one[...]
    out[1] = two[...]


def cross_kernel(place, keep, recv, out):
    out[0] = (keep[0, 0] + recv[0, 0].astype(F32)).astype(BF)


def spread_kernel(place, keep, recv, came, to_a, to_b):
    def mine(b):
        return (keep[0, b] + recv[0, b].astype(F32) + came[b].astype(F32)).astype(BF)

    to_a[...] = mine(0)
    to_b[...] = mine(1)


def total_kernel(place, arrived, kept, came, out):
    @pl.when(ends(place))
    def _():
        out[...] = (arrived[...].astype(F32) + kept[...].astype(F32)).astype(BF)

    @pl.when(jnp.logical_not(ends(place)))
    def _():
        out[...] = (arrived[...].astype(F32) + came[...].astype(F32)).astype(BF)


def panel_kernel(place, anc, tq, inv, out):
    w = inv.shape[0]
    out[...] = dot((anc[...] + tq[:, :w].astype(F32)).astype(BF), inv[...]).astype(BF)


def choose_kernel(place, own, came, out, *, source):
    @pl.when(lax.rem(place[1], source) == 0)
    def _():
        out[...] = own[...]

    @pl.when(lax.rem(place[1], source) != 0)
    def _():
        out[...] = came[...]


def pivot_kernel(place, anc, tq, ty, tc, out):
    for layer, top in ((0, tq), (2, ty), (1, tc.at[0]), (3, tc.at[1])):

        @pl.when(place[2] == layer)
        def _():
            out[...] = (anc[...] + top[...].astype(F32)).astype(BF)


def panel_upper_kernel(place, m, own, other, out):
    out[...] = (dot(m[0], own[...]) + dot(m[1], other[...])).astype(BF)


def upper_kernel(mo_ref, mt_ref, so_ref, st_ref, out_ref):
    total = dot(mo_ref[0, 0], so_ref[0, 0]) + dot(mt_ref[0, 0], st_ref[0, 0])
    out_ref[0, 0] = total.astype(BF)


def make_upper(m_own, m_other, s_own, s_other):
    blocks, pair, half, cw = s_own.shape
    w = m_own.shape[2]
    m_specs = [pl.BlockSpec((1, 1, w, half), lambda k, b, side=side: (side, k, 0, 0)) for side in range(2)]
    s_spec = pl.BlockSpec((1, 1, half, cw), lambda k, b: (b, k, 0, 0))
    return pl.pallas_call(
        upper_kernel,
        grid=(pair, blocks),
        in_specs=[*m_specs, s_spec, s_spec],
        out_specs=pl.BlockSpec((1, 1, w, cw), lambda k, b: (b, k, 0, 0)),
        out_shape=jax.ShapeDtypeStruct((blocks, pair, w, cw), BF),
        cost_estimate=COST,
        compiler_params=pltpu.CompilerParams(vmem_limit_bytes=SMALL),
        name="upper",
    )(m_own, m_other, s_own, s_other)


def product_kernel(place, tiles, low0, low1, up0, up1, keep, send, *, swapped, g, c, nt, rt, ct, tb, pair, tj):
    b, j = pl.program_id(0), pl.program_id(1)
    x, z, l = place[0], place[1], place[2]
    odd = lax.rem(z, 2)
    column = jnp.where(b == 0, jnp.where(odd == 0, jnp.where(z == 0, 1, 0), jnp.where(z == 1, 3, 2)),
                       jnp.where(z == 0, 0, jnp.where(z == 3, 3, 3 - z)))
    column = column * ct + c * tj + j
    for p, flip in enumerate(PIECE):
        i = jnp.bitwise_xor(l, flip)
        rows = pl.ds(pl.multiple_of(i * tb, tb), tb)
        total = None
        for t, low in enumerate((low0, low1)):
            owner = jnp.bitwise_xor(z, t) if swapped else z - odd + t
            for k in range(pair):
                flag = tiles[((owner * pair + k) * nt + x * rt + g * 4 + i) * nt + column]
                left = low[0, k, rows, :] * flag.astype(F32).astype(BF)
                if swapped:
                    right = jnp.where(odd == t, up0[0, k], up1[0, k])
                else:
                    right = (up0, up1)[t][0, k]
                term = dot(left, right)
                total = term if total is None else total + term
        if p < 2:
            keep[p, 0] = total
        else:
            send[p - 2, 0] = total.astype(BF)


def products(place, tiles, lows, up0, up1, *, g, c, nt, rt, ct, tb):
    blocks, pair, w, cw = up0.shape
    tj = cw // tb
    rows = 4 * tb
    up_spec = pl.BlockSpec((1, pair, w, tb), lambda b, j, *_: (b, 0, 0, j))
    out_spec = pl.BlockSpec((2, 1, tb, tb), lambda b, j, *_: (0, b, 0, j))
    one, two, at, swapped = lows
    low_specs = [pl.BlockSpec((1, pair, rows, w), lambda b, j, *_, t=t: (t, 0, at, 0)) for t in (one[1], two[1])]
    return pl.pallas_call(
        functools.partial(product_kernel, swapped=swapped, g=g, c=c, nt=nt, rt=rt, ct=ct, tb=tb, pair=pair, tj=tj),
        grid_spec=pltpu.PrefetchScalarGridSpec(
            num_scalar_prefetch=2,
            grid=(blocks, tj),
            in_specs=[
                *low_specs,
                up_spec,
                up_spec,
            ],
            out_specs=[out_spec, out_spec],
        ),
        out_shape=[
            jax.ShapeDtypeStruct((2, blocks, tb, cw), F32),
            jax.ShapeDtypeStruct((2, blocks, tb, cw), BF),
        ],
        cost_estimate=COST,
        compiler_params=pltpu.CompilerParams(vmem_limit_bytes=MAIN),
        name="products",
    )(place, tiles, one[0], two[0], up0, up1)


def final_kernel(place, tiles, *refs, g, c, nt, rt, ct, tb, tj, first, with_lower):
    anc, tq, ty, tc, au, pq, py, pc = refs[:8]
    outs = refs[8:] if first else refs[8 + (2 if with_lower else 1):]
    p = pl.program_id(0)
    x, z, l = place[0], place[1], place[2]
    flip = jnp.where(p == 0, 0, jnp.where(p == 1, 2, jnp.where(p == 2, 1, 3)))
    i = x * rt + g * 4 + jnp.bitwise_xor(l, flip)

    def work(total, panel):
        if with_lower:
            outs[1][...] = panel
        for j in range(tj):
            cols = slice(j * tb, (j + 1) * tb)
            base = anc[:, cols] + total[:, cols].astype(F32)
            flag = tiles[i * nt + z * ct + c * tj + j] != 0

            @pl.when(flag)
            def _():
                outs[0][:, cols] = base - dot(panel, au[:, cols])

            @pl.when(jnp.logical_not(flag))
            def _():
                outs[0][:, cols] = base

    for q, (t, v) in enumerate(((tq, pq), (ty, py), (tc.at[0], pc.at[0]), (tc.at[1], pc.at[1]))):

        @pl.when(p == q)
        def _():
            work(t[...], v[...])


def final(place, tiles, ancestor, total, au, panel, kept, *, g, c, nt, rt, ct, tb, with_lower):
    rows, cols = ancestor.shape
    tq, ty, tc = total
    pq, py, pc = panel
    cw, w = tq.shape[1], pq.shape[1]
    tj = cw // tb
    first = kept is None

    def whole(shape):
        return pl.BlockSpec(shape, lambda p, *_: (0,) * len(shape))

    def tile_row(p, place):
        flip = jnp.where(p == 0, 0, jnp.where(p == 1, 2, jnp.where(p == 2, 1, 3)))
        return g * 4 + jnp.bitwise_xor(place[2], flip)

    out_specs = [pl.BlockSpec((tb, cw), lambda p, place, *_: (tile_row(p, place), c))]
    out_shape = [jax.ShapeDtypeStruct((rows, cols), F32)]
    if with_lower:
        out_specs.append(pl.BlockSpec((tb, w), lambda p, place, *_: (tile_row(p, place), 0)))
        out_shape.append(jax.ShapeDtypeStruct((rows, w), BF))
    in_specs = [
        pl.BlockSpec((tb, cw), lambda p, place, *_: (tile_row(p, place), c)),
        whole(tq.shape), whole(ty.shape), whole(tc.shape), whole(au.shape),
        whole(pq.shape), whole(py.shape), whole(pc.shape),
    ]
    operands = [ancestor, tq, ty, tc, au, pq, py, pc]
    aliases = {}
    if not first:
        for n in range(len(out_shape)):
            aliases[2 + len(operands)] = n
            operands.append(kept[n])
            in_specs.append(pl.BlockSpec(memory_space=pl.ANY))
    return pl.pallas_call(
        functools.partial(
            final_kernel, g=g, c=c, nt=nt, rt=rt, ct=ct, tb=tb, tj=tj, first=first, with_lower=with_lower
        ),
        grid_spec=pltpu.PrefetchScalarGridSpec(
            num_scalar_prefetch=2, grid=(4,), in_specs=in_specs, out_specs=out_specs
        ),
        out_shape=out_shape,
        input_output_aliases=aliases,
        cost_estimate=COST,
        compiler_params=pltpu.CompilerParams(vmem_limit_bytes=WIDE),
        name="final",
    )(place, tiles, *operands)


def after(value, *earlier):
    return lax.optimization_barrier((value, *earlier))[0]


def paired(
    ancestor, leaf_lower, leaf_upper, leaf_upper_inv, leaf_lower_inv, leaf_pivots, leaf_tiles,
    anc_upper_inv, anc_lower_inv, anc_pivots, anc_tiles, *, order, split,
):
    rows, cols = ancestor.shape
    pair, w = leaf_lower.shape[1], leaf_lower.shape[-1]
    half = leaf_upper.shape[2]
    nt = leaf_tiles.shape[-1]
    tb = order // nt
    rt, ct = rows // tb, cols // tb
    groups, cw = rows // (4 * tb), cols // split
    x, z, l = lax.axis_index("row"), lax.axis_index("col"), lax.axis_index("layer")
    odd = lax.rem(z, 2)
    is_end = (z == 0) | (z == 3)
    near, far = (z // 2) * 2 * pair, (1 - z // 2) * 2 * pair
    place = jnp.stack([x, z, l]).astype(jnp.int32)
    tiles = leaf_tiles.reshape(-1)
    top_tiles = anc_tiles.reshape(-1)
    shape = dict(nt=nt, rt=rt, ct=ct, tb=tb)
    u = leaf_upper[0]
    chunks = sorted(((g, c) for c in range(split) for g in range(groups)), key=lambda gc: (gc[0] > 0, gc[1] * 1.5 + gc[0], gc[0]))
    parts = [(c, t) for c in range(split) for t in range(2)]
    v = {}
    last = [place]

    def ordered(value):
        return after(value, last[0])

    def done(name, value, token=None):
        v[name] = value
        last[0] = value if token is None else token

    def slices(m):
        c, t = parts[m]

        def near_pair(p):
            return p[1] // 2 * 2

        def far_pair(p):
            return 2 - p[1] // 2 * 2

        def one(k, p):
            return (0, jnp.where(ends(p), far_pair(p), near_pair(p)) + t, k, 0, c)

        def two(k, p):
            return (0, jnp.where(ends(p), near_pair(p), far_pair(p)) + t, k, 0, c)

        src = ordered(leaf_upper)
        src = src.reshape((1, src.shape[1] // pair, pair) + src.shape[2:])
        block = (1, 1, 1, half, cw)
        to_a, to_b = step(
            lambda place, i, j, o, q: copy_kernel(place, i.at[0, 0], j.at[0, 0], o.at[0], q.at[0]), "slices", place,
            [src, src], [(pair, half, cw)] * 2, in_specs=[spec(block, one), spec(block, two)],
            out_specs=[spec((1, half, cw), lambda k, p: (k, 0, 0))] * 2, grid=(pair,), vmem=WIDE,
        )
        v["a", m] = lax.ppermute(to_a, "col", [(1, 0), (2, 3), (0, 2), (3, 1)])
        v["b", m] = (to_b, lax.ppermute(to_b, "col", [(1, 2), (2, 1)]))
        last[0] = to_b

    def lower(first, count):
        n = count * 4
        own = step(
            lower_kernel, "lower", place, [ordered(leaf_lower), leaf_upper_inv], [(pair, n * tb, w)],
            in_specs=[
                spec((1, 1, tb, w), lambda k, i, *_: (0, k, first * 4 + i, 0)),
                spec((1, 1, w, w), lambda k, i, *_: (0, k, 0, 0)),
            ],
            out_specs=[spec((1, tb, w), lambda k, i, *_: (k, i, 0))], grid=(pair, n),
        )
        done(("lower", first), own)

    def share(first, count):
        own = v["lower", first]
        got = lax.all_gather(own, "col", axis_index_groups=[[0, 1], [2, 3]], axis=0, tiled=False)
        for g in range(first, first + count):
            v["low", g] = (got, 0), (got, 1), g - first, False

    def exchange(g):
        own = v["lower", g][None]
        v["low", g] = (own, 0), (lax.ppermute(own, "col", BUDDY), 0), 0, True

    def stack(m):
        kept, came = v["b", m]
        own = step(stack_kernel, "stack", place, [ordered(v["a", m]), kept, came], [(2, pair, half, cw)])
        done(("own", m), own)
        v["other", m] = lax.ppermute(own, "row", SWAP)

    def matrices():
        pivots = leaf_pivots.reshape(leaf_pivots.shape[1], 1, w)
        for t in range(2):
            both = step(
                matrix_kernel, "matrix", place, [ordered(leaf_lower_inv), pivots], [(2, pair, w, half)],
                in_specs=[
                    spec((1, 1, w, w), lambda k, p: (0, p[1] // 2 * 2 * pair + t * pair + k, 0, 0)),
                    spec((1, 1, w), lambda k, p: (p[1] // 2 * 2 * pair + t * pair + k, 0, 0)),
                ],
                out_specs=[spec((2, 1, w, half), lambda k, p: (0, k, 0, 0))], grid=(pair,), vmem=WIDE,
            )
            done(("m", t), (both, both), both)
        both = step(
            matrix_kernel, "matrix", place, [ordered(anc_lower_inv), anc_pivots.reshape(1, w)], [(2, w, half)],
        )
        done("anc_m", both, both)

    def upper(m):
        own = ordered(v["own", m])
        done(("upper",) + parts[m], make_upper(*v["m", parts[m][1]], own, v["other", m]))

    def multiply(n):
        g, c = chunks[n]
        keep, send = products(
            place, tiles, v["low", g], ordered(v["upper", c, 0]), v["upper", c, 1], g=g, c=c, **shape
        )
        done(("keep", n), keep, send)
        v["core", n] = lax.ppermute(send, "layer", CORE)

    def cross(n):
        crossing = step(
            cross_kernel, "cross", place, [ordered(v["keep", n]), v["core", n]], [(2, tb, cw)],
            in_specs=[spec((1, 1, tb, cw), lambda b, *_: (1, b, 0, 0))] * 2,
            out_specs=[spec((1, tb, cw), lambda b, *_: (b, 0, 0))], grid=(2,),
        )
        v["y", n] = lax.ppermute(crossing, "layer", YPAIR)
        last[0] = crossing

    def spread(n):
        to_a, to_b = step(
            spread_kernel, "spread", place, [ordered(v["keep", n]), v["core", n], v["y", n]], [(tb, cw)] * 2,
            in_specs=[spec((1, 2, tb, cw))] * 2 + [None], cost=LONG if n else COST,
        )
        v["qa", n] = lax.ppermute(to_a, "col", [(0, 1), (3, 2), (1, 3), (2, 0)])
        v["qb", n] = (to_b, lax.ppermute(to_b, "col", [(1, 2), (2, 1)]))
        last[0] = to_b

    def total(n):
        kept, came = v["qb", n]
        tq = step(total_kernel, "total", place, [ordered(v["qa", n]), kept, came], [(tb, cw)])
        v["ty", n] = lax.ppermute(tq, "layer", YPAIR)
        done(("tq", n), tq)

    def both(one, two):
        return step(pair_kernel, "pair", place, [ordered(one), two], [(2,) + one.shape])

    def gather(n):
        two = both(v["tq", n], v["ty", n])
        v["tc", n] = lax.ppermute(two, "layer", CORE)
        last[0] = two

    def panel(n):
        g, c = chunks[n]
        pq = step(
            panel_kernel, "panel", place, [ancestor, ordered(v["tq", n]), anc_upper_inv], [(tb, w)],
            in_specs=[spec((tb, w), lambda i, p: (g * 4 + p[2], 0)), None, None], vmem=WIDE,
        )
        v["p1", g] = (pq, lax.ppermute(pq, "col", [(0, 2)]))
        last[0] = pq

    def choose(source, own, came):
        return step(
            functools.partial(choose_kernel, source=source), "choose", place, [ordered(own), came], [own.shape]
        )

    def panel_two(n):
        g, c = chunks[n]
        pq = choose(4, *v["p1", g])
        v["p2", g] = (pq, lax.ppermute(pq, "col", [(0, 1), (2, 3)]))
        last[0] = pq

    def panel_y(n):
        g, c = chunks[n]
        pq = choose(2, *v["p2", g])
        v["py", g] = lax.ppermute(pq, "layer", YPAIR)
        done(("pq", g), pq)

    def panel_core(n):
        g, c = chunks[n]
        two = both(v["pq", g], v["py", g])
        v["pc", g] = lax.ppermute(two, "layer", CORE)
        last[0] = two

    def pivot(n):
        g, c = chunks[n]
        rows_own = step(
            pivot_kernel, "pivot", place, [ancestor, ordered(v["tq", n]), v["ty", n], v["tc", n]], [(tb, cw)],
            in_specs=[spec((tb, cw), lambda *_: (0, c)), None, None, None], vmem=WIDE,
        )
        v["pivot", c] = (rows_own, lax.ppermute(rows_own, "row", SWAP))
        last[0] = rows_own

    def pivot_two(n):
        g, c = chunks[n]
        rows_own, rows_other = v["pivot", c]
        done(("anc_upper", c), step(
            panel_upper_kernel, "anc_upper", place, [v["anc_m"], ordered(rows_own), rows_other], [(w, cw)]
        ))

    out = {}

    def finish(n):
        g, c = chunks[n]
        with_lower = c == 0
        kept = None if not out else ((out["schur"], out["lower"]) if with_lower else (out["schur"],))
        made = final(
            place, top_tiles, ancestor, (ordered(v["tq", n]), v["ty", n], v["tc", n]), v["anc_upper", c],
            (v["pq", g], v["py", g], v["pc", g]), kept, g=g, c=c, with_lower=with_lower, **shape,
        )
        out["schur"] = made[0]
        if with_lower:
            out["lower"] = made[1]
        last[0] = made[0]

    slices(0)
    slices(1)
    lower(0, 1)
    share(0, 1)
    slices(2)
    slices(3)
    lower(1, groups - 1)
    matrices()
    stack(0)
    stack(1)
    upper(0)
    last[0] = after(last[0], v["low", 0][0][0])
    v["lower", 1] = after(v["lower", 1], last[0])
    share(1, groups - 1)
    stack(2)
    upper(1)
    work = [(0, 3.5, stack, 3), (1, 1.5, upper, 2), (2, 6.5, upper, 3)]
    for n, (g, c) in enumerate(chunks):
        slot = n + GAP * (n > 0)
        steps = [(0, 0, multiply), (2, 2, total), (1, 2.9, spread), (0, 3, cross), (4, 2.5, gather)]
        if g == 0:
            steps += [(4, 6, pivot), (5, 5, pivot_two)]
        if c == 0:
            steps += [(2, 2.1, panel), (4, 2.6, panel_two), (5, 2.7, panel_y), (6, 2.8, panel_core)]
        steps.append((6 if c == 0 else 5, 7, finish))
        work += [(slot + lag, position, stage, n) for lag, position, stage in steps]
    for _, _, stage, n in sorted(work, key=lambda e: e[:2]):
        stage(n)
    anc_upper = jnp.concatenate([v["anc_upper", c] for c in range(split)], axis=1)
    return out["lower"], anc_upper, out["schur"]


def solution(mesh):
    sizes = mesh.shape

    def shards(*args):
        ancestor, leaf_lower, leaf_upper, leaf_tiles = args[0], args[1], args[2], args[6]
        rows, cols = ancestor.shape
        order = rows * sizes["row"]
        nt = leaf_tiles.shape[-1]
        tb = order // nt
        w, half = leaf_lower.shape[-1], leaf_upper.shape[2]
        fits = (
            (sizes["layer"], sizes["row"], sizes["col"]) == (4, 2, 4)
            and leaf_lower.shape[0] == 1 and leaf_upper.shape[1] == 4 * leaf_lower.shape[1]
            and order % nt == 0 and rows % (4 * tb) == 0 and cols % (2 * tb) == 0
            and half == tb and tb % 128 == 0 and w <= cols // 2
        )
        if fits:
            return paired(*args, order=order, split=2)
        return plain(*args, order=order)

    return jax.shard_map(
        shards,
        mesh=mesh,
        in_specs=(
            P("row", "col"), P("layer", "col", "row", None), P("layer", None, "row", "col"),
            P("layer", "col", None, None), P("layer", None, None, None), P("layer", None, None),
            P("layer", None, None, None), P(), P(), P(), P(),
        ),
        out_specs=(P("row", None), P(None, "col"), P("row", "col")),
        check_vma=False,
    )
```

```python
import functools

import jax
import jax.numpy as jnp
from jax import lax
from jax.experimental import pallas as pl
from jax.experimental.pallas import tpu as pltpu
from jax.sharding import PartitionSpec as P

BF = jnp.bfloat16
F32 = jnp.float32
MIB = 1024 * 1024
GAP = 2
SMALL, MAIN, WIDE = 16 * MIB, 20 * MIB, 48 * MIB
COST = pl.CostEstimate(flops=1, transcendentals=0, bytes_accessed=1)
LONG = pl.CostEstimate(flops=5 * 10**13, transcendentals=0, bytes_accessed=1)
SWAP = [(0, 1), (1, 0)]
CORE = [(0, 1), (1, 0), (2, 3), (3, 2)]
YPAIR = [(0, 2), (2, 0), (1, 3), (3, 1)]
BUDDY = [(0, 1), (1, 0), (2, 3), (3, 2)]
PIECE = (0, 2, 1, 3)


def dot(a, b):
    return jnp.dot(a, b, preferred_element_type=F32)


def plain(
    ancestor, leaf_lower, leaf_upper, leaf_upper_inv, leaf_lower_inv, leaf_pivots, leaf_tiles,
    anc_upper_inv, anc_lower_inv, anc_pivots, anc_tiles, *, order,
):
    row_count, col_count = ancestor.shape
    panel_rows = leaf_upper.shape[2]
    width = leaf_lower.shape[-1]
    nt = leaf_tiles.shape[-1]
    tb = order // nt

    def onehot_tiles(first, count):
        tile = (first + jnp.arange(count, dtype=jnp.int32)) // tb
        return (tile[:, None] == jnp.arange(nt, dtype=jnp.int32)[None, :]).astype(F32)

    row_onehot = onehot_tiles(lax.axis_index("row") * row_count, row_count)
    col_onehot = onehot_tiles(lax.axis_index("col") * col_count, col_count)
    rows_all = lax.all_gather(leaf_upper[0], "row", axis=1, tiled=True)
    permuted = jnp.take_along_axis(rows_all, leaf_pivots[0][:, :, None], axis=1)
    upper_all = jnp.einsum("kij,kjc->kic", leaf_lower_inv[0], permuted, preferred_element_type=F32).astype(BF)
    own_lower = jnp.einsum("jrw,jwv->jrv", leaf_lower[0], leaf_upper_inv[0], preferred_element_type=F32).astype(BF)
    masks = jnp.einsum("rt,mts,cs->mrc", row_onehot, leaf_tiles[0].astype(F32), col_onehot)
    products = jnp.einsum(
        "mrw,mwc->mrc", lax.all_gather(own_lower, "col", axis=0, tiled=True), upper_all, preferred_element_type=F32
    )
    a_sum = ancestor + lax.psum(jnp.sum(masks * products, axis=0), "layer")
    gathered = lax.all_gather(a_sum[:panel_rows].astype(BF), "row", axis=0, tiled=True)
    anc_upper = dot(anc_lower_inv, jnp.take(gathered, anc_pivots, axis=0)).astype(BF)
    panel = dot(a_sum[:, :width].astype(BF), anc_upper_inv).astype(BF)
    kept = jnp.where(lax.axis_index("col") == 0, panel, 0).astype(BF)
    anc_lower = lax.psum(kept, "col")
    anc_mask = jnp.einsum("rt,ts,cs->rc", row_onehot, anc_tiles.astype(F32), col_onehot)
    return anc_lower, anc_upper, a_sum - anc_mask * dot(anc_lower, anc_upper)


def spec(shape, index=None):
    if index is None:
        return pl.BlockSpec(shape, lambda *_: (0,) * len(shape))
    return pl.BlockSpec(shape, index)


def step(body, name, place, operands, outs, *, in_specs=None, out_specs=None, grid=(1,), cost=COST, vmem=SMALL):
    in_specs = in_specs or [None] * len(operands)
    in_specs = [spec(o.shape) if i is None else i for o, i in zip(operands, in_specs)]
    out_specs = out_specs or [spec(o) for o in outs]
    made = pl.pallas_call(
        body,
        grid_spec=pltpu.PrefetchScalarGridSpec(
            num_scalar_prefetch=1, grid=grid, in_specs=in_specs, out_specs=out_specs
        ),
        out_shape=[jax.ShapeDtypeStruct(o, BF) for o in outs],
        cost_estimate=cost,
        compiler_params=pltpu.CompilerParams(vmem_limit_bytes=vmem),
        name=name,
    )(place, *operands)
    return made if len(made) > 1 else made[0]


def ends(place):
    return (place[1] == 0) | (place[1] == 3)


def copy_kernel(place, one, two, to_a, to_b):
    to_a[...] = one[0]
    to_b[...] = two[0]


def matrix_kernel(place, inv, pivots, out):
    half = out.shape[-1]
    for side in range(2):
        first = jnp.bitwise_xor(place[0], side) * half
        wanted = first + lax.broadcasted_iota(jnp.int32, (half, inv.shape[-1]), 0)
        picks = (wanted == pivots[...].reshape(1, -1)).astype(F32).astype(BF)
        product = lax.dot_general(
            inv[...].reshape(inv.shape[-2:]), picks, (((1,), (1,)), ((), ())), preferred_element_type=F32
        )
        out[side, ...] = product.astype(BF).reshape(out.shape[1:])


def lower_kernel(place, low, inv, out):
    out[0] = dot(low[0, 0], inv[0, 0]).astype(BF)


def stack_kernel(place, first, kept, came, out):
    out[0] = first[...]

    @pl.when(ends(place))
    def _():
        out[1] = kept[...]

    @pl.when(jnp.logical_not(ends(place)))
    def _():
        out[1] = came[...]


def pair_kernel(place, one, two, out):
    out[0] = one[...]
    out[1] = two[...]


def cross_kernel(place, keep, recv, out):
    out[0] = (keep[0, 0] + recv[0, 0].astype(F32)).astype(BF)


def spread_kernel(place, keep, recv, came, to_a, to_b):
    def mine(b):
        return (keep[0, b] + recv[0, b].astype(F32) + came[b].astype(F32)).astype(BF)

    to_a[...] = mine(0)
    to_b[...] = mine(1)


def total_kernel(place, arrived, kept, came, out):
    @pl.when(ends(place))
    def _():
        out[...] = (arrived[...].astype(F32) + kept[...].astype(F32)).astype(BF)

    @pl.when(jnp.logical_not(ends(place)))
    def _():
        out[...] = (arrived[...].astype(F32) + came[...].astype(F32)).astype(BF)


def panel_kernel(place, anc, tq, inv, out):
    w = inv.shape[0]
    out[...] = dot((anc[...] + tq[:, :w].astype(F32)).astype(BF), inv[...]).astype(BF)


def choose_kernel(place, own, came, out, *, source):
    @pl.when(lax.rem(place[1], source) == 0)
    def _():
        out[...] = own[...]

    @pl.when(lax.rem(place[1], source) != 0)
    def _():
        out[...] = came[...]


def pivot_kernel(place, anc, tq, ty, tc, out):
    for layer, top in ((0, tq), (2, ty), (1, tc.at[0]), (3, tc.at[1])):

        @pl.when(place[2] == layer)
        def _():
            out[...] = (anc[...] + top[...].astype(F32)).astype(BF)


def panel_upper_kernel(place, m, own, other, out):
    out[...] = (dot(m[0], own[...]) + dot(m[1], other[...])).astype(BF)


def upper_kernel(mo_ref, mt_ref, so_ref, st_ref, out_ref):
    total = dot(mo_ref[0, 0], so_ref[0, 0]) + dot(mt_ref[0, 0], st_ref[0, 0])
    out_ref[0, 0] = total.astype(BF)


def make_upper(m_own, m_other, s_own, s_other):
    blocks, pair, half, cw = s_own.shape
    w = m_own.shape[2]
    m_specs = [pl.BlockSpec((1, 1, w, half), lambda k, b, side=side: (side, k, 0, 0)) for side in range(2)]
    s_spec = pl.BlockSpec((1, 1, half, cw), lambda k, b: (b, k, 0, 0))
    return pl.pallas_call(
        upper_kernel,
        grid=(pair, blocks),
        in_specs=[*m_specs, s_spec, s_spec],
        out_specs=pl.BlockSpec((1, 1, w, cw), lambda k, b: (b, k, 0, 0)),
        out_shape=jax.ShapeDtypeStruct((blocks, pair, w, cw), BF),
        cost_estimate=COST,
        compiler_params=pltpu.CompilerParams(vmem_limit_bytes=SMALL),
        name="upper",
    )(m_own, m_other, s_own, s_other)


def product_kernel(place, tiles, low0, low1, up0, up1, keep, send, *, swapped, g, c, nt, rt, ct, tb, pair, tj):
    b, j = pl.program_id(0), pl.program_id(1)
    x, z, l = place[0], place[1], place[2]
    odd = lax.rem(z, 2)
    column = jnp.where(b == 0, jnp.where(odd == 0, jnp.where(z == 0, 1, 0), jnp.where(z == 1, 3, 2)),
                       jnp.where(z == 0, 0, jnp.where(z == 3, 3, 3 - z)))
    column = column * ct + c * tj + j
    for p, flip in enumerate(PIECE):
        i = jnp.bitwise_xor(l, flip)
        rows = pl.ds(pl.multiple_of(i * tb, tb), tb)
        total = None
        for t, low in enumerate((low0, low1)):
            owner = jnp.bitwise_xor(z, t) if swapped else z - odd + t
            for k in range(pair):
                flag = tiles[((owner * pair + k) * nt + x * rt + g * 4 + i) * nt + column]
                left = low[0, k, rows, :] * flag.astype(F32).astype(BF)
                if swapped:
                    right = jnp.where(odd == t, up0[0, k], up1[0, k])
                else:
                    right = (up0, up1)[t][0, k]
                term = dot(left, right)
                total = term if total is None else total + term
        if p < 2:
            keep[p, 0] = total
        else:
            send[p - 2, 0] = total.astype(BF)


def products(place, tiles, lows, up0, up1, *, g, c, nt, rt, ct, tb):
    blocks, pair, w, cw = up0.shape
    tj = cw // tb
    rows = 4 * tb
    up_spec = pl.BlockSpec((1, pair, w, tb), lambda b, j, *_: (b, 0, 0, j))
    out_spec = pl.BlockSpec((2, 1, tb, tb), lambda b, j, *_: (0, b, 0, j))
    one, two, at, swapped = lows
    low_specs = [pl.BlockSpec((1, pair, rows, w), lambda b, j, *_, t=t: (t, 0, at, 0)) for t in (one[1], two[1])]
    return pl.pallas_call(
        functools.partial(product_kernel, swapped=swapped, g=g, c=c, nt=nt, rt=rt, ct=ct, tb=tb, pair=pair, tj=tj),
        grid_spec=pltpu.PrefetchScalarGridSpec(
            num_scalar_prefetch=2,
            grid=(blocks, tj),
            in_specs=[
                *low_specs,
                up_spec,
                up_spec,
            ],
            out_specs=[out_spec, out_spec],
        ),
        out_shape=[
            jax.ShapeDtypeStruct((2, blocks, tb, cw), F32),
            jax.ShapeDtypeStruct((2, blocks, tb, cw), BF),
        ],
        cost_estimate=COST,
        compiler_params=pltpu.CompilerParams(vmem_limit_bytes=MAIN),
        name="products",
    )(place, tiles, one[0], two[0], up0, up1)


def final_kernel(place, tiles, *refs, g, c, nt, rt, ct, tb, tj, first, with_lower):
    anc, tq, ty, tc, au, pq, py, pc = refs[:8]
    outs = refs[8:] if first else refs[8 + (2 if with_lower else 1):]
    p = pl.program_id(0)
    x, z, l = place[0], place[1], place[2]
    flip = jnp.where(p == 0, 0, jnp.where(p == 1, 2, jnp.where(p == 2, 1, 3)))
    i = x * rt + g * 4 + jnp.bitwise_xor(l, flip)

    def work(total, panel):
        if with_lower:
            outs[1][...] = panel
        for j in range(tj):
            cols = slice(j * tb, (j + 1) * tb)
            base = anc[:, cols] + total[:, cols].astype(F32)
            flag = tiles[i * nt + z * ct + c * tj + j] != 0

            @pl.when(flag)
            def _():
                outs[0][:, cols] = base - dot(panel, au[:, cols])

            @pl.when(jnp.logical_not(flag))
            def _():
                outs[0][:, cols] = base

    for q, (t, v) in enumerate(((tq, pq), (ty, py), (tc.at[0], pc.at[0]), (tc.at[1], pc.at[1]))):

        @pl.when(p == q)
        def _():
            work(t[...], v[...])


def final(place, tiles, ancestor, total, au, panel, kept, *, g, c, nt, rt, ct, tb, with_lower):
    rows, cols = ancestor.shape
    tq, ty, tc = total
    pq, py, pc = panel
    cw, w = tq.shape[1], pq.shape[1]
    tj = cw // tb
    first = kept is None

    def whole(shape):
        return pl.BlockSpec(shape, lambda p, *_: (0,) * len(shape))

    def tile_row(p, place):
        flip = jnp.where(p == 0, 0, jnp.where(p == 1, 2, jnp.where(p == 2, 1, 3)))
        return g * 4 + jnp.bitwise_xor(place[2], flip)

    out_specs = [pl.BlockSpec((tb, cw), lambda p, place, *_: (tile_row(p, place), c))]
    out_shape = [jax.ShapeDtypeStruct((rows, cols), F32)]
    if with_lower:
        out_specs.append(pl.BlockSpec((tb, w), lambda p, place, *_: (tile_row(p, place), 0)))
        out_shape.append(jax.ShapeDtypeStruct((rows, w), BF))
    in_specs = [
        pl.BlockSpec((tb, cw), lambda p, place, *_: (tile_row(p, place), c)),
        whole(tq.shape), whole(ty.shape), whole(tc.shape), whole(au.shape),
        whole(pq.shape), whole(py.shape), whole(pc.shape),
    ]
    operands = [ancestor, tq, ty, tc, au, pq, py, pc]
    aliases = {}
    if not first:
        for n in range(len(out_shape)):
            aliases[2 + len(operands)] = n
            operands.append(kept[n])
            in_specs.append(pl.BlockSpec(memory_space=pl.ANY))
    return pl.pallas_call(
        functools.partial(
            final_kernel, g=g, c=c, nt=nt, rt=rt, ct=ct, tb=tb, tj=tj, first=first, with_lower=with_lower
        ),
        grid_spec=pltpu.PrefetchScalarGridSpec(
            num_scalar_prefetch=2, grid=(4,), in_specs=in_specs, out_specs=out_specs
        ),
        out_shape=out_shape,
        input_output_aliases=aliases,
        cost_estimate=COST,
        compiler_params=pltpu.CompilerParams(vmem_limit_bytes=WIDE),
        name="final",
    )(place, tiles, *operands)


def after(value, *earlier):
    return lax.optimization_barrier((value, *earlier))[0]


def paired(
    ancestor, leaf_lower, leaf_upper, leaf_upper_inv, leaf_lower_inv, leaf_pivots, leaf_tiles,
    anc_upper_inv, anc_lower_inv, anc_pivots, anc_tiles, *, order, split,
):
    rows, cols = ancestor.shape
    pair, w = leaf_lower.shape[1], leaf_lower.shape[-1]
    half = leaf_upper.shape[2]
    nt = leaf_tiles.shape[-1]
    tb = order // nt
    rt, ct = rows // tb, cols // tb
    groups, cw = rows // (4 * tb), cols // split
    x, z, l = lax.axis_index("row"), lax.axis_index("col"), lax.axis_index("layer")
    odd = lax.rem(z, 2)
    is_end = (z == 0) | (z == 3)
    near, far = (z // 2) * 2 * pair, (1 - z // 2) * 2 * pair
    place = jnp.stack([x, z, l]).astype(jnp.int32)
    tiles = leaf_tiles.reshape(-1)
    top_tiles = anc_tiles.reshape(-1)
    shape = dict(nt=nt, rt=rt, ct=ct, tb=tb)
    u = leaf_upper[0]
    chunks = sorted(((g, c) for c in range(split) for g in range(groups)), key=lambda gc: (gc[0] > 0, gc[1] * 1.5 + gc[0], gc[0]))
    parts = [(c, t) for c in range(split) for t in range(2)]
    v = {}
    last = [place]

    def ordered(value):
        return after(value, last[0])

    def done(name, value, token=None):
        v[name] = value
        last[0] = value if token is None else token

    def slices(m):
        c, t = parts[m]

        def near_pair(p):
            return p[1] // 2 * 2

        def far_pair(p):
            return 2 - p[1] // 2 * 2

        def one(k, p):
            return (0, jnp.where(ends(p), far_pair(p), near_pair(p)) + t, k, 0, c)

        def two(k, p):
            return (0, jnp.where(ends(p), near_pair(p), far_pair(p)) + t, k, 0, c)

        src = ordered(leaf_upper)
        src = src.reshape((1, src.shape[1] // pair, pair) + src.shape[2:])
        block = (1, 1, 1, half, cw)
        to_a, to_b = step(
            lambda place, i, j, o, q: copy_kernel(place, i.at[0, 0], j.at[0, 0], o.at[0], q.at[0]), "slices", place,
            [src, src], [(pair, half, cw)] * 2, in_specs=[spec(block, one), spec(block, two)],
            out_specs=[spec((1, half, cw), lambda k, p: (k, 0, 0))] * 2, grid=(pair,), vmem=WIDE,
        )
        v["a", m] = lax.ppermute(to_a, "col", [(1, 0), (2, 3), (0, 2), (3, 1)])
        v["b", m] = (to_b, lax.ppermute(to_b, "col", [(1, 2), (2, 1)]))
        last[0] = to_b

    def lower(first, count):
        n = count * 4
        own = step(
            lower_kernel, "lower", place, [ordered(leaf_lower), leaf_upper_inv], [(pair, n * tb, w)],
            in_specs=[
                spec((1, 1, tb, w), lambda k, i, *_: (0, k, first * 4 + i, 0)),
                spec((1, 1, w, w), lambda k, i, *_: (0, k, 0, 0)),
            ],
            out_specs=[spec((1, tb, w), lambda k, i, *_: (k, i, 0))], grid=(pair, n),
        )
        done(("lower", first), own)

    def share(first, count):
        own = v["lower", first]
        got = lax.all_gather(own, "col", axis_index_groups=[[0, 1], [2, 3]], axis=0, tiled=False)
        for g in range(first, first + count):
            v["low", g] = (got, 0), (got, 1), g - first, False

    def exchange(g):
        own = v["lower", g][None]
        v["low", g] = (own, 0), (lax.ppermute(own, "col", BUDDY), 0), 0, True

    def stack(m):
        kept, came = v["b", m]
        own = step(stack_kernel, "stack", place, [ordered(v["a", m]), kept, came], [(2, pair, half, cw)])
        done(("own", m), own)
        v["other", m] = lax.ppermute(own, "row", SWAP)

    def matrices():
        pivots = leaf_pivots.reshape(leaf_pivots.shape[1], 1, w)
        for t in range(2):
            both = step(
                matrix_kernel, "matrix", place, [ordered(leaf_lower_inv), pivots], [(2, pair, w, half)],
                in_specs=[
                    spec((1, 1, w, w), lambda k, p: (0, p[1] // 2 * 2 * pair + t * pair + k, 0, 0)),
                    spec((1, 1, w), lambda k, p: (p[1] // 2 * 2 * pair + t * pair + k, 0, 0)),
                ],
                out_specs=[spec((2, 1, w, half), lambda k, p: (0, k, 0, 0))], grid=(pair,), vmem=WIDE,
            )
            done(("m", t), (both, both), both)
        both = step(
            matrix_kernel, "matrix", place, [ordered(anc_lower_inv), anc_pivots.reshape(1, w)], [(2, w, half)],
        )
        done("anc_m", both, both)

    def upper(m):
        own = ordered(v["own", m])
        done(("upper",) + parts[m], make_upper(*v["m", parts[m][1]], own, v["other", m]))

    def multiply(n):
        g, c = chunks[n]
        keep, send = products(
            place, tiles, v["low", g], ordered(v["upper", c, 0]), v["upper", c, 1], g=g, c=c, **shape
        )
        done(("keep", n), keep, send)
        v["core", n] = lax.ppermute(send, "layer", CORE)

    def cross(n):
        crossing = step(
            cross_kernel, "cross", place, [ordered(v["keep", n]), v["core", n]], [(2, tb, cw)],
            in_specs=[spec((1, 1, tb, cw), lambda b, *_: (1, b, 0, 0))] * 2,
            out_specs=[spec((1, tb, cw), lambda b, *_: (b, 0, 0))], grid=(2,),
        )
        v["y", n] = lax.ppermute(crossing, "layer", YPAIR)
        last[0] = crossing

    def spread(n):
        to_a, to_b = step(
            spread_kernel, "spread", place, [ordered(v["keep", n]), v["core", n], v["y", n]], [(tb, cw)] * 2,
            in_specs=[spec((1, 2, tb, cw))] * 2 + [None], cost=LONG if n else COST,
        )
        v["qa", n] = lax.ppermute(to_a, "col", [(0, 1), (3, 2), (1, 3), (2, 0)])
        v["qb", n] = (to_b, lax.ppermute(to_b, "col", [(1, 2), (2, 1)]))
        last[0] = to_b

    def total(n):
        kept, came = v["qb", n]
        tq = step(total_kernel, "total", place, [ordered(v["qa", n]), kept, came], [(tb, cw)])
        v["ty", n] = lax.ppermute(tq, "layer", YPAIR)
        done(("tq", n), tq)

    def both(one, two):
        return step(pair_kernel, "pair", place, [ordered(one), two], [(2,) + one.shape])

    def gather(n):
        two = both(v["tq", n], v["ty", n])
        v["tc", n] = lax.ppermute(two, "layer", CORE)
        last[0] = two

    def panel(n):
        g, c = chunks[n]
        pq = step(
            panel_kernel, "panel", place, [ancestor, ordered(v["tq", n]), anc_upper_inv], [(tb, w)],
            in_specs=[spec((tb, w), lambda i, p: (g * 4 + p[2], 0)), None, None], vmem=WIDE,
        )
        v["p1", g] = (pq, lax.ppermute(pq, "col", [(0, 2)]))
        last[0] = pq

    def choose(source, own, came):
        return step(
            functools.partial(choose_kernel, source=source), "choose", place, [ordered(own), came], [own.shape]
        )

    def panel_two(n):
        g, c = chunks[n]
        pq = choose(4, *v["p1", g])
        v["p2", g] = (pq, lax.ppermute(pq, "col", [(0, 1), (2, 3)]))
        last[0] = pq

    def panel_y(n):
        g, c = chunks[n]
        pq = choose(2, *v["p2", g])
        v["py", g] = lax.ppermute(pq, "layer", YPAIR)
        done(("pq", g), pq)

    def panel_core(n):
        g, c = chunks[n]
        two = both(v["pq", g], v["py", g])
        v["pc", g] = lax.ppermute(two, "layer", CORE)
        last[0] = two

    def pivot(n):
        g, c = chunks[n]
        rows_own = step(
            pivot_kernel, "pivot", place, [ancestor, ordered(v["tq", n]), v["ty", n], v["tc", n]], [(tb, cw)],
            in_specs=[spec((tb, cw), lambda *_: (0, c)), None, None, None], vmem=WIDE,
        )
        v["pivot", c] = (rows_own, lax.ppermute(rows_own, "row", SWAP))
        last[0] = rows_own

    def pivot_two(n):
        g, c = chunks[n]
        rows_own, rows_other = v["pivot", c]
        done(("anc_upper", c), step(
            panel_upper_kernel, "anc_upper", place, [v["anc_m"], ordered(rows_own), rows_other], [(w, cw)]
        ))

    out = {}

    def finish(n):
        g, c = chunks[n]
        with_lower = c == 0
        kept = None if not out else ((out["schur"], out["lower"]) if with_lower else (out["schur"],))
        made = final(
            place, top_tiles, ancestor, (ordered(v["tq", n]), v["ty", n], v["tc", n]), v["anc_upper", c],
            (v["pq", g], v["py", g], v["pc", g]), kept, g=g, c=c, with_lower=with_lower, **shape,
        )
        out["schur"] = made[0]
        if with_lower:
            out["lower"] = made[1]
        last[0] = made[0]

    slices(0)
    slices(1)
    lower(0, 1)
    share(0, 1)
    slices(2)
    slices(3)
    lower(1, groups - 1)
    matrices()
    stack(0)
    stack(1)
    upper(0)
    last[0] = after(last[0], v["low", 0][0][0])
    v["lower", 1] = after(v["lower", 1], last[0])
    share(1, groups - 1)
    stack(2)
    upper(1)
    work = [(0, 3.5, stack, 3), (1, 1.5, upper, 2), (2, 6.5, upper, 3)]
    for n, (g, c) in enumerate(chunks):
        slot = n + GAP * (n > 0)
        soon = int(n == len(chunks) - 3)
        steps = [(0, 0, multiply), (2, 2, total), (1, 2.9, spread), (0, 3, cross), (4, 2.5, gather)]
        if g == 0:
            steps += [(4, 6, pivot), (5, 5, pivot_two)]
        if c == 0:
            steps += [(2, 2.1, panel), (4 - soon, 2.6 + 2 * soon, panel_two), (5 - soon, 2.7 + 2 * soon, panel_y),
                (6 - soon, 2.8 + 2 * soon, panel_core)]
        steps.append((6 - soon if c == 0 else 5, 7, finish))
        work += [(slot + lag, position, stage, n) for lag, position, stage in steps]
    for _, _, stage, n in sorted(work, key=lambda e: e[:2]):
        stage(n)
    anc_upper = jnp.concatenate([v["anc_upper", c] for c in range(split)], axis=1)
    return out["lower"], anc_upper, out["schur"]


def solution(mesh):
    sizes = mesh.shape

    def shards(*args):
        ancestor, leaf_lower, leaf_upper, leaf_tiles = args[0], args[1], args[2], args[6]
        rows, cols = ancestor.shape
        order = rows * sizes["row"]
        nt = leaf_tiles.shape[-1]
        tb = order // nt
        w, half = leaf_lower.shape[-1], leaf_upper.shape[2]
        fits = (
            (sizes["layer"], sizes["row"], sizes["col"]) == (4, 2, 4)
            and leaf_lower.shape[0] == 1 and leaf_upper.shape[1] == 4 * leaf_lower.shape[1]
            and order % nt == 0 and rows % (4 * tb) == 0 and cols % (2 * tb) == 0
            and half == tb and tb % 128 == 0 and w <= cols // 2
        )
        if fits:
            return paired(*args, order=order, split=2)
        return plain(*args, order=order)

    return jax.shard_map(
        shards,
        mesh=mesh,
        in_specs=(
            P("row", "col"), P("layer", "col", "row", None), P("layer", None, "row", "col"),
            P("layer", "col", None, None), P("layer", None, None, None), P("layer", None, None),
            P("layer", None, None, None), P(), P(), P(), P(),
        ),
        out_specs=(P("row", None), P(None, "col"), P("row", "col")),
        check_vma=False,
    )
```
